32 devices in a mesh: ctx: 16 (over z, y, x), heads: 2 (over core).
Axes of the slice: x: 2, y: 2, z: 4, core: 2. Of those that a mesh axis runs over, the one named last changes fastest.
Arguments:
- ssm_input: bfloat16 [3072, 8192], P('ctx', 'heads'), may hold values from -36 to 36
- gate_input: bfloat16 [3072, 8192], P('ctx', 'heads'), may hold values from -6 to 6
- write_proj: bfloat16 [3072, 128], P('ctx'), may hold values from -0.5 to 0.5
- read_proj: bfloat16 [3072, 128], P('ctx'), may hold values from -0.5 to 0.5
- log_decay: float32 [3072, 128], P('ctx', 'heads'), may hold values from -0.75 to 0, as said below
- skip_gain: float32 [128], P('heads'), may hold values from 0.5 to 2
- norm_gain: float32 [8192], P('heads'), may hold values from 0.1 to 1.9
- query_rows: bfloat16 [3072, 4096], P('ctx', 'heads'), may hold values from -6 to 6
- key_rows: bfloat16 [3072, 1024], P('ctx', 'heads'), may hold values from -6 to 6
- value_rows: bfloat16 [3072, 1024], P('ctx', 'heads'), may hold values from -6 to 6
Outputs:
- ssm_out: bfloat16 [3072, 8192], P('ctx', 'heads')
- attn_out: bfloat16 [3072, 4096], P('ctx', 'heads')
The draws below stay inside these ranges and needn't reach their ends.
Inputs may be any that keep to these rules, and one draw needn't show every extreme that they name: `log_decay`: negative everywhere.
All inputs are finite; a program needn't handle non-finite values.
Results may differ from the reference program's by a relative error of at most 0.0075.
Values may be sent and summed in bfloat16 or wider, within the bound.
A program may use at most 128 MiB of HBM per device.

```python
import math
import jax
import jax.numpy as jnp
from jax import lax

SSM_HEADS = 128
HEAD_P = 64
STATE = 128
QUERY_HEADS = 32
KV_HEADS = 8
HEAD_DIM = 128
SPAN = 64
TOK_DEV = 192
SEQUENCE_TOKENS = 3072


def draw_ssm_input(key, part):
    split_random_keys = jax.random.split(key, 3)
    width_all = SSM_HEADS * HEAD_P
    basis = jnp.clip(jax.random.normal(split_random_keys[0], (SEQUENCE_TOKENS, width_all), jnp.float32), -3.0, 3.0)
    head_place = (jnp.arange(width_all) // HEAD_P).astype(jnp.float32) / max(SSM_HEADS - 1, 1)
    column_scale = jnp.exp(jax.random.uniform(split_random_keys[1], (width_all,), jnp.float32, math.log(0.25), math.log(2.5)))
    column_scale = column_scale * (1.0 + head_place)
    row_scale = jnp.exp(jax.random.uniform(split_random_keys[2], (SEQUENCE_TOKENS, 1), jnp.float32, math.log(0.5), math.log(1.6)))
    return (basis * column_scale[None, :] * row_scale).astype(jnp.bfloat16)


def draw_log_decay(key, part):
    split_random_keys = jax.random.split(key, 7)
    keep_share = 0.5
    slow_heads = jax.random.uniform(split_random_keys[0], (SSM_HEADS,), jnp.float32) < keep_share
    slow_rate = jnp.exp(jax.random.uniform(split_random_keys[1], (SSM_HEADS,), jnp.float32, math.log(0.15), math.log(0.6))) / SEQUENCE_TOKENS
    fast_rate = jnp.exp(jax.random.uniform(split_random_keys[2], (SSM_HEADS,), jnp.float32, math.log(0.04), math.log(0.07)))
    per_head_rate = jnp.where(slow_heads, slow_rate, fast_rate)
    block_count = SEQUENCE_TOKENS // TOK_DEV
    block_factor = jnp.exp(jax.random.uniform(split_random_keys[3], (block_count,), jnp.float32, math.log(0.5), math.log(2.0)))
    row_index_list = jnp.arange(SEQUENCE_TOKENS)
    row_multiplier = block_factor[row_index_list // TOK_DEV]
    jaggedness_measure = jax.random.uniform(split_random_keys[4], (SEQUENCE_TOKENS, SSM_HEADS), jnp.float32, 0.5, 1.5)
    spike_row_values = jax.random.randint(split_random_keys[5], (3,), 0, SEQUENCE_TOKENS)
    spike_penalty = jax.random.uniform(split_random_keys[6], (3,), jnp.float32, 0.22, 0.5)
    spike_sum_total = jnp.sum(jnp.where(row_index_list[:, None] == spike_row_values[None, :], spike_penalty[None, :], 0.0), axis=1)
    return -(per_head_rate[None, :] * row_multiplier[:, None] * jaggedness_measure) - spike_sum_total[:, None]


def drawn_rows(key, width_all):
    return jnp.clip(jax.random.normal(key, (SEQUENCE_TOKENS, width_all), jnp.float32), -6.0, 6.0)


def draw_query_rows(key, part):
    basis = drawn_rows(jax.random.fold_in(key, 1), QUERY_HEADS * HEAD_DIM)
    return basis.astype(jnp.bfloat16)


def draw_key_rows(key, part):
    basis = drawn_rows(jax.random.fold_in(key, 2), KV_HEADS * HEAD_DIM)
    return basis.astype(jnp.bfloat16)


def shard_levels(stream_key, extent, cuts, smallest, top_value):
    def one(axis_at, parts):
        steps = jax.random.uniform(jax.random.fold_in(jax.random.fold_in(stream_key, 6), axis_at), (parts,), jnp.float32, smallest / len(cuts), top_value / len(cuts))
        return jnp.repeat(jnp.exp(steps), extent[axis_at] // parts).reshape((-1,) + (1,) * (len(extent) - axis_at - 1))

    factor_of = one(*cuts[0])
    for cut in cuts[1:]:
        factor_of = factor_of * one(*cut)
    return factor_of


def gaussian(stream_key, dims, deviation, bound, cuts=(), held_as=jnp.bfloat16):
    factor_of = shard_levels(stream_key, dims, cuts, -0.22, 0.18) if cuts else 1.0
    values = jax.random.normal(stream_key, dims, jnp.float32) * deviation * factor_of
    return jnp.minimum(jnp.maximum(values, -bound), bound).astype(held_as)


def setup_inputs(seed: int = 0) -> dict:
    arg_keys = jax.random.split(jax.random.key(seed), 11)
    return {
        "ssm_input": draw_ssm_input(jax.random.fold_in(arg_keys[10], 71), 0),
        "gate_input": gaussian(arg_keys[1], (SEQUENCE_TOKENS, SSM_HEADS * HEAD_P), 1.0, 6.0, ((0, 16), (1, 2))),
        "write_proj": gaussian(arg_keys[2], (SEQUENCE_TOKENS, STATE), STATE ** -0.5, 0.5, ((0, 16),)),
        "read_proj": gaussian(arg_keys[3], (SEQUENCE_TOKENS, STATE), STATE ** -0.5, 0.5, ((0, 16),)),
        "log_decay": draw_log_decay(jax.random.fold_in(arg_keys[10], 71), 0),
        "skip_gain": jnp.clip(0.5 + 1.5 * jax.random.uniform(arg_keys[5], (SSM_HEADS,), jnp.float32) ** shard_levels(arg_keys[5], (SSM_HEADS,), ((0, 2),), -0.2, 0.2), 0.5, 2.0),
        "norm_gain": jnp.clip(1.0 + 0.18 * jax.random.normal(arg_keys[6], (SSM_HEADS * HEAD_P,), jnp.float32), 0.1, 1.9),
        "query_rows": draw_query_rows(jax.random.fold_in(arg_keys[10], 71), 0),
        "key_rows": draw_key_rows(jax.random.fold_in(arg_keys[10], 71), 0),
        "value_rows": gaussian(arg_keys[9], (SEQUENCE_TOKENS, KV_HEADS * HEAD_DIM), 1.0, 6.0, ((0, 16), (1, 2))),
    }


def state_mixer(ssm_input, gate_input, write_proj, read_proj, log_decay, skip_gain, norm_gain):
    block_count = SEQUENCE_TOKENS // SPAN
    inputs_blk = ssm_input.reshape(block_count, SPAN, SSM_HEADS, HEAD_P)
    write_blk = write_proj.reshape(block_count, SPAN, STATE)
    read_blk = read_proj.reshape(block_count, SPAN, STATE)
    decay_blk = log_decay.reshape(block_count, SPAN, SSM_HEADS)
    causal = jnp.arange(SPAN)[:, None] >= jnp.arange(SPAN)[None, :]

    def span_step(state_in, block_item):
        x_block, write_block, read_block, decay_block = block_item
        cum_decay = jnp.cumsum(decay_block, axis=0)
        cum_heads = cum_decay.T
        decay_gap = cum_heads[:, :, None] - cum_heads[:, None, :]
        decay_mask = jnp.where(causal[None], jnp.exp(jnp.where(causal[None], decay_gap, 0.0)), 0.0)
        intersection = jnp.dot(read_block, write_block.T, preferred_element_type=jnp.float32)
        mix_weights = intersection[None] * decay_mask
        x_float = x_block.astype(jnp.float32)
        y_local = jnp.einsum('hts,shp->thp', mix_weights, x_float, precision=lax.Precision.HIGHEST)
        tail_decay = jnp.exp(cum_heads[:, -1:] - cum_heads)
        weighted_write = tail_decay[:, :, None] * write_block.astype(jnp.float32)[None]
        block_state = jnp.einsum('shp,hsn->hpn', x_float, weighted_write, precision=lax.Precision.HIGHEST)
        y_carry = jnp.einsum('tn,hpn->thp', read_block.astype(jnp.float32), state_in, precision=lax.Precision.HIGHEST) * jnp.exp(cum_decay)[:, :, None]
        mixed_out = y_local + y_carry + skip_gain[None, :, None] * x_float
        state_out = jnp.exp(cum_heads[:, -1])[:, None, None] * state_in + block_state
        return (state_out, mixed_out)
    state_zero = jnp.zeros((SSM_HEADS, HEAD_P, STATE), jnp.float32)
    _, mixed_all = lax.scan(span_step, state_zero, (inputs_blk, write_blk, read_blk, decay_blk))
    mixed_all = mixed_all.reshape(SEQUENCE_TOKENS, SSM_HEADS * HEAD_P)
    gated = mixed_all * jax.nn.silu(gate_input.astype(jnp.float32))
    mean_square = lax.optimization_barrier(jnp.mean(gated * gated, axis=1, keepdims=True))
    return (gated * lax.rsqrt(mean_square + 1e-05) * norm_gain[None, :]).astype(jnp.bfloat16)

def attention(query_rows, key_rows, value_rows):
    group_size = QUERY_HEADS // KV_HEADS
    scale_factor = 1.0 / HEAD_DIM ** 0.5
    queries_all = query_rows.reshape(SEQUENCE_TOKENS, QUERY_HEADS, HEAD_DIM)
    keys_all = key_rows.reshape(SEQUENCE_TOKENS, KV_HEADS, HEAD_DIM)
    values_all = value_rows.reshape(SEQUENCE_TOKENS, KV_HEADS, HEAD_DIM)
    block_total = SEQUENCE_TOKENS // TOK_DEV
    key_positions = jnp.arange(SEQUENCE_TOKENS, dtype=jnp.int32)

    def one_block(flat_index):
        head_index = flat_index // block_total
        block_index = flat_index % block_total
        first_row = (block_index * TOK_DEV).astype(jnp.int32)
        query_block = lax.dynamic_slice_in_dim(queries_all, first_row, TOK_DEV, 0)
        query_block = lax.dynamic_index_in_dim(query_block, head_index, 1, keepdims=False)
        kv_index = (head_index // group_size).astype(jnp.int32)
        key_head = lax.dynamic_index_in_dim(keys_all, kv_index, 1, keepdims=False)
        value_head = lax.dynamic_index_in_dim(values_all, kv_index, 1, keepdims=False)
        scores = jnp.dot(query_block, key_head.T, preferred_element_type=jnp.float32) * scale_factor
        query_positions = first_row + jnp.arange(TOK_DEV, dtype=jnp.int32)
        visible = key_positions[None, :] <= query_positions[:, None]
        row_max = lax.optimization_barrier(jnp.max(jnp.where(visible, scores, -jnp.inf), axis=1, keepdims=True))
        weights = jnp.where(visible, jnp.exp(jnp.where(visible, scores - row_max, 0.0)), 0.0)
        weight_sum = lax.optimization_barrier(jnp.sum(weights, axis=1, keepdims=True))
        result = jnp.dot(weights.astype(jnp.bfloat16), value_head, preferred_element_type=jnp.float32) / weight_sum
        return result.astype(jnp.bfloat16)
    blocks_out = lax.map(one_block, jnp.arange(QUERY_HEADS * block_total, dtype=jnp.int32))
    blocks_out = blocks_out.reshape(QUERY_HEADS, block_total, TOK_DEV, HEAD_DIM)
    return jnp.transpose(blocks_out, (1, 2, 0, 3)).reshape(SEQUENCE_TOKENS, QUERY_HEADS * HEAD_DIM)

def reference(ssm_input, gate_input, write_proj, read_proj, log_decay, skip_gain, norm_gain, query_rows, key_rows, value_rows):
    ssm_out = state_mixer(ssm_input, gate_input, write_proj, read_proj, log_decay, skip_gain, norm_gain)
    attn_out = attention(query_rows, key_rows, value_rows)
    return (ssm_out, attn_out)
```

```python
import functools
import math

import jax
import jax.numpy as jnp
from jax import lax
from jax.experimental import pallas as pl
from jax.experimental.pallas import tpu as pltpu
from jax.sharding import PartitionSpec as P

SSM_HEADS = 128
HEAD_P = 64
STATE = 128
QUERY_HEADS = 32
KV_HEADS = 8
HEAD_DIM = 128
SPAN = 64


def carried_in(part, axis, combine, identity):
    place = lax.axis_index(axis)
    gathered = jax.tree.map(lambda a: lax.all_gather(a, axis), part)
    state = jax.tree.map(lambda a, e: jnp.zeros_like(a) + jnp.asarray(e, a.dtype), part, identity)

    def one(step, state):
        return combine(
            state, jax.tree.map(lambda a: lax.dynamic_index_in_dim(a, step, 0, False), gathered)
        )

    return lax.fori_loop(0, place, one, state)


def chain_combine(earlier, later):
    return (earlier[0] * later[0], later[0][:, None, None] * earlier[1] + later[1])


def local_mixer(ssm_input, gate_input, write_proj, read_proj, log_decay, skip_gain, norm_gain):
    row_count, width_local = ssm_input.shape
    head_local = log_decay.shape[1]
    block_count = row_count // SPAN
    inputs_blk = ssm_input.reshape(block_count, SPAN, head_local, HEAD_P)
    inputs_float = inputs_blk.astype(jnp.float32)
    write_blk = write_proj.reshape(block_count, SPAN, STATE)
    read_blk = read_proj.reshape(block_count, SPAN, STATE)
    cum_decay = jnp.cumsum(log_decay.reshape(block_count, SPAN, head_local), axis=1)
    cum_heads = jnp.transpose(cum_decay, (0, 2, 1))
    causal = jnp.arange(SPAN)[:, None] >= jnp.arange(SPAN)[None, :]
    decay_gap = cum_heads[:, :, :, None] - cum_heads[:, :, None, :]
    decay_mask = jnp.where(causal, jnp.exp(jnp.where(causal, decay_gap, 0.0)), 0.0)
    intersection = jnp.einsum(
        "ctn,csn->cts", read_blk, write_blk, preferred_element_type=jnp.float32
    )
    mix_weights = intersection[:, None] * decay_mask
    y_local = jnp.einsum(
        "chts,cshp->cthp", mix_weights, inputs_float, precision=lax.Precision.HIGHEST
    )
    tail_decay = jnp.exp(cum_heads[:, :, -1:] - cum_heads)
    weighted_write = tail_decay[:, :, :, None] * write_blk[:, None].astype(jnp.float32)
    block_state = jnp.einsum(
        "cshp,chsn->chpn", inputs_float, weighted_write, precision=lax.Precision.HIGHEST
    )
    block_decay = jnp.exp(cum_heads[:, :, -1])

    def prefix_step(carry_in, block_item):
        return (chain_combine(carry_in, block_item), carry_in)

    start_pair = (
        jnp.ones((head_local,), jnp.float32),
        jnp.zeros((head_local, HEAD_P, STATE), jnp.float32),
    )
    device_pair, prefix_pair = lax.scan(prefix_step, start_pair, (block_decay, block_state))
    incoming = carried_in(device_pair, "ctx", chain_combine, start_pair)
    start_state = prefix_pair[0][:, :, None, None] * incoming[1][None] + prefix_pair[1]
    y_carry = (
        jnp.einsum(
            "ctn,chpn->cthp",
            read_blk.astype(jnp.float32),
            start_state,
            precision=lax.Precision.HIGHEST,
        )
        * jnp.exp(cum_decay)[:, :, :, None]
    )
    mixed_out = y_local + y_carry + skip_gain[None, None, :, None] * inputs_float
    gated = mixed_out.reshape(row_count, width_local) * jax.nn.silu(gate_input.astype(jnp.float32))
    square_total = lax.psum(jnp.sum(gated * gated, axis=1), "heads")
    row_scale = lax.rsqrt(square_total / (SSM_HEADS * HEAD_P) + 1e-05)
    return (gated * row_scale[:, None] * norm_gain[None, :]).astype(jnp.bfloat16)


def attend_block(
    state, query_block, query_positions, top_position, key_block, value_block, first_key
):
    scale_factor = 1.0 / HEAD_DIM**0.5
    key_count = key_block.shape[0]

    def compute(state_in):
        running_max, running_sum, running_acc = state_in
        scores = (
            jnp.einsum("gqd,ngd->gqn", query_block, key_block, preferred_element_type=jnp.float32)
            * scale_factor
        )
        key_positions = first_key + jnp.arange(key_count, dtype=jnp.int32)
        visible = key_positions[None, None, :] <= query_positions[None, :, None]
        block_max = jnp.max(jnp.where(visible, scores, -1e30), axis=2)
        new_max = jnp.maximum(running_max, block_max)
        weights = jnp.where(
            visible, jnp.exp(jnp.where(visible, scores - new_max[:, :, None], 0.0)), 0.0
        )
        rescale = jnp.exp(running_max - new_max)
        new_sum = rescale * running_sum + jnp.sum(weights, axis=2)
        new_acc = rescale[:, :, None] * running_acc + jnp.einsum(
            "gqn,ngd->gqd",
            weights.astype(jnp.bfloat16),
            value_block,
            preferred_element_type=jnp.float32,
        )
        return (new_max, new_sum, new_acc)

    return lax.cond(first_key > top_position, lambda state_in: state_in, compute, state)


def attention_local(query_rows, key_rows, value_rows):
    row_count = query_rows.shape[0]
    head_sets = key_rows.shape[1] // HEAD_DIM
    group_size = QUERY_HEADS // KV_HEADS
    own_index = lax.axis_index("ctx")
    query_stack = query_rows.reshape(row_count, head_sets, group_size, HEAD_DIM)
    query_stack = jnp.transpose(query_stack, (1, 0, 2, 3)).reshape(
        head_sets, row_count * group_size, HEAD_DIM
    )
    stacked_rows = jnp.arange(row_count * group_size, dtype=jnp.int32) // group_size
    own_positions = own_index * row_count + stacked_rows
    query_sets = [(query_stack, own_positions)]
    tops = [jnp.max(positions) for _, positions in query_sets]
    carries = tuple(
        (
            (
                jnp.full((head_sets, block.shape[1]), -1e30, jnp.float32),
                jnp.zeros((head_sets, block.shape[1]), jnp.float32),
                jnp.zeros((head_sets, block.shape[1], HEAD_DIM), jnp.float32),
            )
            for block, _ in query_sets
        )
    )
    key_piece = lax.all_gather(key_rows, "ctx", axis=0, tiled=True)
    value_piece = lax.all_gather(value_rows, "ctx", axis=0, tiled=True)
    piece_rows = key_piece.shape[0]
    key_blocks = key_piece.reshape(piece_rows // row_count, row_count, head_sets, HEAD_DIM)
    value_blocks = value_piece.reshape(piece_rows // row_count, row_count, head_sets, HEAD_DIM)
    offsets = row_count * jnp.arange(piece_rows // row_count, dtype=jnp.int32)

    def inner_step(states, block_item):
        key_block, value_block, first_key = block_item
        updated = tuple(
            (
                attend_block(
                    states[number],
                    query_sets[number][0],
                    query_sets[number][1],
                    tops[number],
                    key_block,
                    value_block,
                    first_key,
                )
                for number in range(len(query_sets))
            )
        )
        return (updated, None)

    result, _ = lax.scan(inner_step, carries, (key_blocks, value_blocks, offsets))
    finished = [(state[2] / state[1][:, :, None]).astype(jnp.bfloat16) for state in result]
    combined = finished[0]
    combined = combined.reshape(head_sets, row_count, group_size, HEAD_DIM)
    return jnp.transpose(combined, (1, 0, 2, 3)).reshape(
        row_count, head_sets * group_size * HEAD_DIM
    )


def body(
    ssm_input,
    gate_input,
    write_proj,
    read_proj,
    log_decay,
    skip_gain,
    norm_gain,
    query_rows,
    key_rows,
    value_rows,
):
    ssm_out = local_mixer(
        ssm_input, gate_input, write_proj, read_proj, log_decay, skip_gain, norm_gain
    )
    attn_out = attention_local(query_rows, key_rows, value_rows)
    return (ssm_out, attn_out)


GROUP = 4
WIDE = 8
F32 = jnp.float32
BF16 = jnp.bfloat16
LOG2E = math.log2(math.e)


def expand_heads(per_head):
    shape = (WIDE, WIDE * HEAD_P)
    first = lax.broadcasted_iota(jnp.int32, shape, 0) * HEAD_P
    column = lax.broadcasted_iota(jnp.int32, shape, 1)
    spread = jnp.where((column >= first) & (column < first + HEAD_P), 1.0, 0.0).astype(BF16)
    high = per_head.astype(BF16)
    low = (per_head - high.astype(F32)).astype(BF16)
    return jnp.dot(high, spread, preferred_element_type=F32) + jnp.dot(
        low, spread, preferred_element_type=F32
    )


def state_kernel(x_ref, write_ref, cum_ref, out_ref):
    cum = cum_ref[0]
    rows = cum.shape[0]
    weight = expand_heads(jnp.exp(cum[rows - 1 :, :] - cum))
    scaled = (x_ref[...].astype(F32) * weight).astype(BF16)
    out_ref[...] = lax.dot_general(
        scaled, write_ref[...], (((0,), (0,)), ((), ())), preferred_element_type=F32
    ).astype(BF16)


def local_kernel(x_ref, write_ref, read_ref, cum_ref, cum_t_ref, skip_ref, out_ref):
    rows = x_ref.shape[0]
    inner = lax.dot_general(
        read_ref[...], write_ref[...], (((1,), (1,)), ((), ())), preferred_element_type=F32
    )
    later = lax.broadcasted_iota(jnp.int32, (rows, rows), 0)
    earlier = lax.broadcasted_iota(jnp.int32, (rows, rows), 1)
    inner = jnp.where(earlier <= later, inner, 0.0)
    cum = cum_ref[0]
    cum_t = cum_t_ref[...]
    left = lax.broadcasted_iota(jnp.int32, (rows, 2 * HEAD_P), 1) < HEAD_P
    for pair in range(WIDE // 2):
        columns = slice(pair * 2 * HEAD_P, (pair + 1) * 2 * HEAD_P)
        x_pair = x_ref[:, columns]
        halves = []
        for h in (2 * pair, 2 * pair + 1):
            gap = cum[:, h : h + 1] - cum_t[h : h + 1, :]
            mix = (jnp.exp(jnp.minimum(gap, 0.0)) * inner).astype(BF16)
            halves.append(jnp.dot(mix, x_pair, preferred_element_type=F32))
        mixed = jnp.where(left, halves[0], halves[1])
        out_ref[:, columns] = mixed + skip_ref[:, columns] * x_pair.astype(F32)


def gate_kernel(part_ref, gate_ref, read_ref, cum_ref, start_ref, out_ref, square_ref):
    carry = lax.dot_general(
        read_ref[...], start_ref[...], (((1,), (1,)), ((), ())), preferred_element_type=F32
    )
    gate = gate_ref[...].astype(F32)
    mixed = part_ref[...] + expand_heads(jnp.exp(cum_ref[0])) * carry
    gated = mixed * (gate / (1.0 + jnp.exp(-gate)))
    out_ref[...] = gated
    square = gated * gated
    total = square[:, :128]
    for k in range(1, square.shape[1] // 128):
        total = total + square[:, k * 128 : (k + 1) * 128]

    @pl.when(pl.program_id(0) == 0)
    def _():
        square_ref[...] = total

    @pl.when(pl.program_id(0) > 0)
    def _():
        square_ref[...] += total


def attend_kernel(rows, first, last, *refs):
    info_ref, q_ref, kv_ref = refs[:3]
    state_in = refs[3 : 3 + (0 if first else 3)]
    outs = refs[3 + len(state_in) :]
    factor = LOG2E / math.sqrt(HEAD_DIM)
    heads = q_ref.shape[2] // HEAD_DIM
    key_count = GROUP * rows
    block = pl.program_id(0)
    place = info_ref[0]

    def finish(h, new_max, new_sum, new_acc):
        if last:
            total = jnp.sum(new_sum, axis=1, keepdims=True)
            outs[0][0, :, h * HEAD_DIM : (h + 1) * HEAD_DIM] = (new_acc / total).astype(BF16)
        else:
            outs[0][0, h] = jnp.broadcast_to(new_max, (rows, HEAD_DIM))
            outs[1][0, h] = new_sum
            outs[2][0, h] = new_acc

    def compute():
        keys = kv_ref[:, :, :HEAD_DIM].reshape(key_count, HEAD_DIM)
        values = kv_ref[:, :, HEAD_DIM:].reshape(key_count, HEAD_DIM)
        if first:
            column = lax.broadcasted_iota(jnp.int32, (1, key_count), 1)
            shift = (place - 0) * rows
            for j in range(1, GROUP):
                shift = jnp.where(column >= j * rows, ((place ^ j) - j) * rows, shift)
            row = lax.broadcasted_iota(jnp.int32, (rows, 1), 0) + (place ^ block) * rows
            visible = column + shift <= row
        for h in range(heads):
            query = q_ref[0, :, h * HEAD_DIM : (h + 1) * HEAD_DIM]
            scores = lax.dot_general(
                query, keys, (((1,), (1,)), ((), ())), preferred_element_type=F32
            )
            if first:
                scores = jnp.where(visible, scores, -1e30)
            new_max = jnp.max(scores, axis=1, keepdims=True)
            if not first:
                new_max = jnp.maximum(new_max, state_in[0][0, h][:, :1])
            weights = jnp.exp2((scores - new_max) * factor)
            new_sum = weights[:, :HEAD_DIM]
            for k in range(1, key_count // HEAD_DIM):
                new_sum = new_sum + weights[:, k * HEAD_DIM : (k + 1) * HEAD_DIM]
            new_acc = jnp.dot(weights.astype(BF16), values, preferred_element_type=F32)
            if not first:
                rescale = jnp.exp2((state_in[0][0, h] - new_max) * factor)
                new_sum = new_sum + rescale * state_in[1][0, h]
                new_acc = new_acc + rescale * state_in[2][0, h]
            finish(h, new_max, new_sum, new_acc)

    if first:
        compute()
    else:
        seen = info_ref[1] > 0
        pl.when(seen)(compute)

        @pl.when(jnp.logical_not(seen))
        def _():
            for h in range(heads):
                finish(h, state_in[0][0, h][:, :1], state_in[1][0, h], state_in[2][0, h])


def attend_step(info, query, keys_values, state, last):
    first = state is None
    rows, width = query.shape[1:]
    heads = width // HEAD_DIM
    state_shape = jax.ShapeDtypeStruct((GROUP, heads, rows, HEAD_DIM), F32)
    state_spec = pl.BlockSpec((1, heads, rows, HEAD_DIM), lambda i: (i, 0, 0, 0))
    query_spec = pl.BlockSpec((1, rows, width), lambda i: (i, 0, 0))
    return pl.pallas_call(
        functools.partial(attend_kernel, rows, first, last),
        grid=(GROUP,),
        in_specs=[
            pl.BlockSpec(memory_space=pltpu.SMEM),
            query_spec,
            pl.BlockSpec(keys_values.shape, lambda i: (0, 0, 0)),
        ]
        + ([] if first else [state_spec] * 3),
        out_specs=query_spec if last else [state_spec] * 3,
        out_shape=jax.ShapeDtypeStruct(query.shape, BF16) if last else [state_shape] * 3,
        compiler_params=pltpu.CompilerParams(vmem_limit_bytes=40 * 2**20),
        cost_estimate=pl.CostEstimate(
            flops=4 * GROUP * heads * rows * GROUP * rows * HEAD_DIM,
            bytes_accessed=12 * 2**20,
            transcendentals=GROUP * heads * rows * GROUP * rows,
        ),
        name="attend",
    )(info, query, keys_values, *(() if first else state))


def grouped_body(
    ctx_size,
    ssm_input,
    gate_input,
    write_proj,
    read_proj,
    log_decay,
    skip_gain,
    norm_gain,
    query_rows,
    key_rows,
    value_rows,
):
    rows, width = ssm_input.shape
    head_local = log_decay.shape[1]
    steps = head_local // WIDE
    block = WIDE * HEAD_P
    groups = ctx_size // GROUP
    own = lax.axis_index("ctx")
    place = lax.rem(own, GROUP)
    level = lax.div(own, GROUP)

    def swap(piece, j):
        return lax.ppermute(piece, "ctx", [(i, i ^ j) for i in range(ctx_size)])

    def upward(piece):
        pairs = [(i, i + GROUP) for i in range(ctx_size - GROUP)]
        return jax.tree.map(lambda a: lax.ppermute(a, "ctx", pairs), piece)

    def pick(pieces, index):
        return lax.dynamic_index_in_dim(pieces, index, 0, False)

    def trade(pick_for):
        return [
            pick_for(place ^ j) if j == 0 else swap(pick_for(place ^ j), j) for j in range(GROUP)
        ]

    key_sets = key_rows.shape[1] // GROUP
    query_sets = query_rows.shape[1] // GROUP

    def part_of(array, size, index):
        return lax.dynamic_slice_in_dim(array, index * size, size, 1)

    keys_values = jnp.stack(
        trade(
            lambda p: jnp.concatenate(
                [part_of(key_rows, key_sets, p), part_of(value_rows, key_sets, p)], axis=1
            )
        )
    )
    query = jnp.stack(trade(lambda p: part_of(query_rows, query_sets, p)))

    causal = (jnp.arange(rows)[:, None] >= jnp.arange(rows)[None, :]).astype(F32)
    cum = jnp.dot(causal, log_decay, precision=lax.Precision.HIGHEST)
    cum_blocks = jnp.transpose(cum.reshape(rows, steps, WIDE), (1, 0, 2))
    cum_t = cum.T
    x_spec = pl.BlockSpec((rows, block), lambda i: (0, i))
    proj_spec = pl.BlockSpec((rows, STATE), lambda i: (0, 0))
    cum_spec = pl.BlockSpec((1, rows, WIDE), lambda i: (i, 0, 0))
    state_spec = pl.BlockSpec((block, STATE), lambda i: (i, 0))
    row_spec = pl.BlockSpec((1, block), lambda i: (0, i))
    own_state = pl.pallas_call(
        state_kernel,
        grid=(steps,),
        in_specs=[x_spec, proj_spec, cum_spec],
        out_specs=state_spec,
        out_shape=jax.ShapeDtypeStruct((width, STATE), BF16),
        cost_estimate=pl.CostEstimate(
            flops=2 * rows * width * STATE, bytes_accessed=4 * 2**20, transcendentals=rows * width
        ),
        name="own_state",
    )(ssm_input, write_proj, cum_blocks)
    quarter = head_local // GROUP
    own_states = own_state.reshape(GROUP, quarter, HEAD_P, STATE)
    own_decays = jnp.exp(cum[rows - 1]).reshape(GROUP, quarter)
    states = jnp.stack(trade(lambda p: pick(own_states, p)))
    decays = jnp.stack(trade(lambda p: pick(own_decays, p)))

    part = pl.pallas_call(
        local_kernel,
        grid=(steps,),
        in_specs=[
            x_spec,
            proj_spec,
            proj_spec,
            cum_spec,
            pl.BlockSpec((WIDE, rows), lambda i: (i, 0)),
            row_spec,
        ],
        out_specs=x_spec,
        out_shape=jax.ShapeDtypeStruct((rows, width), F32),
        compiler_params=pltpu.CompilerParams(vmem_limit_bytes=40 * 2**20),
        cost_estimate=pl.CostEstimate(
            flops=4 * rows * rows * width,
            bytes_accessed=6 * 2**20,
            transcendentals=rows * rows * head_local,
        ),
        name="mix_local",
    )(ssm_input, write_proj, read_proj, cum_blocks, cum_t, jnp.repeat(skip_gain, HEAD_P)[None])

    in_order = [
        (pick(decays, place ^ k)[:, None, None], pick(states, place ^ k).astype(F32))
        for k in range(GROUP)
    ]
    group_decay, group_state = in_order[0]
    for decay, state in in_order[1:]:
        group_decay, group_state = group_decay * decay, decay * group_state + state
    before = jnp.zeros((quarter, HEAD_P, STATE), BF16)
    for _ in range(groups - 1):
        before = upward((group_decay * before.astype(F32) + group_state).astype(BF16))
    prefix = [before.astype(F32)]
    for decay, state in in_order[:-1]:
        prefix.append(decay * prefix[-1] + state)
    prefix = jnp.stack(prefix).astype(BF16)
    back = jnp.stack(trade(lambda p: pick(prefix, p)))
    start = jnp.concatenate([pick(back, place ^ g) for g in range(GROUP)])
    gated, squares = pl.pallas_call(
        gate_kernel,
        grid=(steps,),
        in_specs=[x_spec, x_spec, proj_spec, cum_spec, state_spec],
        out_specs=[x_spec, proj_spec],
        out_shape=[
            jax.ShapeDtypeStruct((rows, width), F32),
            jax.ShapeDtypeStruct((rows, 128), F32),
        ],
        compiler_params=pltpu.CompilerParams(vmem_limit_bytes=40 * 2**20),
        cost_estimate=pl.CostEstimate(
            flops=2 * rows * width * STATE, bytes_accessed=10 * 2**20, transcendentals=rows * width
        ),
        name="carry_and_gate",
    )(part, gate_input, read_proj, cum_blocks, start.reshape(width, STATE))
    own_square = jnp.sum(squares, axis=1)
    square_total = own_square + lax.ppermute(own_square, "heads", [(0, 1), (1, 0)])
    row_scale = lax.rsqrt(square_total / (SSM_HEADS * HEAD_P) + 1e-05)
    ssm_out = (gated * row_scale[:, None] * norm_gain[None, :]).astype(BF16)

    state = None
    for step in range(groups):
        info = jnp.stack([place, (level >= step).astype(jnp.int32)]).astype(jnp.int32)
        following = upward(keys_values) if step < groups - 1 else None
        state = attend_step(info, query, keys_values, state, step == groups - 1)
        keys_values = following
    outs = trade(lambda p: pick(state, place ^ p))
    outs = jnp.stack(outs)
    attn_out = jnp.concatenate([pick(outs, place ^ g) for g in range(GROUP)], axis=1)
    return (ssm_out, attn_out)


def solution(mesh):
    in_specs = (
        P("ctx", "heads"),
        P("ctx", "heads"),
        P("ctx", None),
        P("ctx", None),
        P("ctx", "heads"),
        P("heads"),
        P("heads"),
        P("ctx", "heads"),
        P("ctx", "heads"),
        P("ctx", "heads"),
    )
    out_specs = (P("ctx", "heads"), P("ctx", "heads"))
    ctx, heads = mesh.shape["ctx"], mesh.shape["heads"]
    grouped = ctx % GROUP == 0 and ctx > GROUP and KV_HEADS // heads == GROUP and heads == 2
    chosen = functools.partial(grouped_body, ctx) if grouped else body
    return jax.shard_map(chosen, mesh=mesh, in_specs=in_specs, out_specs=out_specs, check_vma=False)
```

```python
import functools
import math

import jax
import jax.numpy as jnp
from jax import lax
from jax.experimental import pallas as pl
from jax.experimental.pallas import tpu as pltpu
from jax.sharding import PartitionSpec as P

SSM_HEADS = 128
HEAD_P = 64
STATE = 128
QUERY_HEADS = 32
KV_HEADS = 8
HEAD_DIM = 128
SPAN = 64


def carried_in(part, axis, combine, identity):
    place = lax.axis_index(axis)
    gathered = jax.tree.map(lambda a: lax.all_gather(a, axis), part)
    state = jax.tree.map(lambda a, e: jnp.zeros_like(a) + jnp.asarray(e, a.dtype), part, identity)

    def one(step, state):
        return combine(
            state, jax.tree.map(lambda a: lax.dynamic_index_in_dim(a, step, 0, False), gathered)
        )

    return lax.fori_loop(0, place, one, state)


def chain_combine(earlier, later):
    return (earlier[0] * later[0], later[0][:, None, None] * earlier[1] + later[1])


def local_mixer(ssm_input, gate_input, write_proj, read_proj, log_decay, skip_gain, norm_gain):
    row_count, width_local = ssm_input.shape
    head_local = log_decay.shape[1]
    block_count = row_count // SPAN
    inputs_blk = ssm_input.reshape(block_count, SPAN, head_local, HEAD_P)
    inputs_float = inputs_blk.astype(jnp.float32)
    write_blk = write_proj.reshape(block_count, SPAN, STATE)
    read_blk = read_proj.reshape(block_count, SPAN, STATE)
    cum_decay = jnp.cumsum(log_decay.reshape(block_count, SPAN, head_local), axis=1)
    cum_heads = jnp.transpose(cum_decay, (0, 2, 1))
    causal = jnp.arange(SPAN)[:, None] >= jnp.arange(SPAN)[None, :]
    decay_gap = cum_heads[:, :, :, None] - cum_heads[:, :, None, :]
    decay_mask = jnp.where(causal, jnp.exp(jnp.where(causal, decay_gap, 0.0)), 0.0)
    intersection = jnp.einsum(
        "ctn,csn->cts", read_blk, write_blk, preferred_element_type=jnp.float32
    )
    mix_weights = intersection[:, None] * decay_mask
    y_local = jnp.einsum(
        "chts,cshp->cthp", mix_weights, inputs_float, precision=lax.Precision.HIGHEST
    )
    tail_decay = jnp.exp(cum_heads[:, :, -1:] - cum_heads)
    weighted_write = tail_decay[:, :, :, None] * write_blk[:, None].astype(jnp.float32)
    block_state = jnp.einsum(
        "cshp,chsn->chpn", inputs_float, weighted_write, precision=lax.Precision.HIGHEST
    )
    block_decay = jnp.exp(cum_heads[:, :, -1])

    def prefix_step(carry_in, block_item):
        return (chain_combine(carry_in, block_item), carry_in)

    start_pair = (
        jnp.ones((head_local,), jnp.float32),
        jnp.zeros((head_local, HEAD_P, STATE), jnp.float32),
    )
    device_pair, prefix_pair = lax.scan(prefix_step, start_pair, (block_decay, block_state))
    incoming = carried_in(device_pair, "ctx", chain_combine, start_pair)
    start_state = prefix_pair[0][:, :, None, None] * incoming[1][None] + prefix_pair[1]
    y_carry = (
        jnp.einsum(
            "ctn,chpn->cthp",
            read_blk.astype(jnp.float32),
            start_state,
            precision=lax.Precision.HIGHEST,
        )
        * jnp.exp(cum_decay)[:, :, :, None]
    )
    mixed_out = y_local + y_carry + skip_gain[None, None, :, None] * inputs_float
    gated = mixed_out.reshape(row_count, width_local) * jax.nn.silu(gate_input.astype(jnp.float32))
    square_total = lax.psum(jnp.sum(gated * gated, axis=1), "heads")
    row_scale = lax.rsqrt(square_total / (SSM_HEADS * HEAD_P) + 1e-05)
    return (gated * row_scale[:, None] * norm_gain[None, :]).astype(jnp.bfloat16)


def attend_block(
    state, query_block, query_positions, top_position, key_block, value_block, first_key
):
    scale_factor = 1.0 / HEAD_DIM**0.5
    key_count = key_block.shape[0]

    def compute(state_in):
        running_max, running_sum, running_acc = state_in
        scores = (
            jnp.einsum("gqd,ngd->gqn", query_block, key_block, preferred_element_type=jnp.float32)
            * scale_factor
        )
        key_positions = first_key + jnp.arange(key_count, dtype=jnp.int32)
        visible = key_positions[None, None, :] <= query_positions[None, :, None]
        block_max = jnp.max(jnp.where(visible, scores, -1e30), axis=2)
        new_max = jnp.maximum(running_max, block_max)
        weights = jnp.where(
            visible, jnp.exp(jnp.where(visible, scores - new_max[:, :, None], 0.0)), 0.0
        )
        rescale = jnp.exp(running_max - new_max)
        new_sum = rescale * running_sum + jnp.sum(weights, axis=2)
        new_acc = rescale[:, :, None] * running_acc + jnp.einsum(
            "gqn,ngd->gqd",
            weights.astype(jnp.bfloat16),
            value_block,
            preferred_element_type=jnp.float32,
        )
        return (new_max, new_sum, new_acc)

    return lax.cond(first_key > top_position, lambda state_in: state_in, compute, state)


def attention_local(query_rows, key_rows, value_rows):
    row_count = query_rows.shape[0]
    head_sets = key_rows.shape[1] // HEAD_DIM
    group_size = QUERY_HEADS // KV_HEADS
    own_index = lax.axis_index("ctx")
    query_stack = query_rows.reshape(row_count, head_sets, group_size, HEAD_DIM)
    query_stack = jnp.transpose(query_stack, (1, 0, 2, 3)).reshape(
        head_sets, row_count * group_size, HEAD_DIM
    )
    stacked_rows = jnp.arange(row_count * group_size, dtype=jnp.int32) // group_size
    own_positions = own_index * row_count + stacked_rows
    query_sets = [(query_stack, own_positions)]
    tops = [jnp.max(positions) for _, positions in query_sets]
    carries = tuple(
        (
            (
                jnp.full((head_sets, block.shape[1]), -1e30, jnp.float32),
                jnp.zeros((head_sets, block.shape[1]), jnp.float32),
                jnp.zeros((head_sets, block.shape[1], HEAD_DIM), jnp.float32),
            )
            for block, _ in query_sets
        )
    )
    key_piece = lax.all_gather(key_rows, "ctx", axis=0, tiled=True)
    value_piece = lax.all_gather(value_rows, "ctx", axis=0, tiled=True)
    piece_rows = key_piece.shape[0]
    key_blocks = key_piece.reshape(piece_rows // row_count, row_count, head_sets, HEAD_DIM)
    value_blocks = value_piece.reshape(piece_rows // row_count, row_count, head_sets, HEAD_DIM)
    offsets = row_count * jnp.arange(piece_rows // row_count, dtype=jnp.int32)

    def inner_step(states, block_item):
        key_block, value_block, first_key = block_item
        updated = tuple(
            (
                attend_block(
                    states[number],
                    query_sets[number][0],
                    query_sets[number][1],
                    tops[number],
                    key_block,
                    value_block,
                    first_key,
                )
                for number in range(len(query_sets))
            )
        )
        return (updated, None)

    result, _ = lax.scan(inner_step, carries, (key_blocks, value_blocks, offsets))
    finished = [(state[2] / state[1][:, :, None]).astype(jnp.bfloat16) for state in result]
    combined = finished[0]
    combined = combined.reshape(head_sets, row_count, group_size, HEAD_DIM)
    return jnp.transpose(combined, (1, 0, 2, 3)).reshape(
        row_count, head_sets * group_size * HEAD_DIM
    )


def body(
    ssm_input,
    gate_input,
    write_proj,
    read_proj,
    log_decay,
    skip_gain,
    norm_gain,
    query_rows,
    key_rows,
    value_rows,
):
    ssm_out = local_mixer(
        ssm_input, gate_input, write_proj, read_proj, log_decay, skip_gain, norm_gain
    )
    attn_out = attention_local(query_rows, key_rows, value_rows)
    return (ssm_out, attn_out)


GROUP = 4
WIDE = 8
BLOCK = WIDE * HEAD_P
CHAIN = 4
F32 = jnp.float32
BF16 = jnp.bfloat16
LOG2E = math.log2(math.e)
MESH = pl.DeviceIdType.MESH


def xor_place(a, b):
    a1, a0, b1, b0 = a // 2, a % 2, b // 2, b % 2
    return 2 * (a1 + b1 - 2 * a1 * b1) + (a0 + b0 - 2 * a0 * b0)


def lanes(start, size):
    return pl.ds(pl.multiple_of(start, 128), size)


def expand_heads(per_head):
    first = lax.broadcasted_iota(jnp.int32, (WIDE, BLOCK), 0) * HEAD_P
    column = lax.broadcasted_iota(jnp.int32, (WIDE, BLOCK), 1)
    spread = jnp.where((column >= first) & (column < first + HEAD_P), 1.0, 0.0).astype(BF16)
    high = per_head.astype(BF16)
    low = (per_head - high.astype(F32)).astype(BF16)
    return jnp.dot(high, spread, preferred_element_type=F32) + jnp.dot(
        low, spread, preferred_element_type=F32
    )


def grouped_kernel(
    groups,
    x_ref,
    gate_ref,
    write_ref,
    read_ref,
    cum_ref,
    cum_t_ref,
    skip_ref,
    gain_ref,
    query_ref,
    key_ref,
    value_ref,
    ssm_ref,
    attn_ref,
    kv_buf,
    q_buf,
    o_buf,
    own_states,
    states,
    own_decays,
    decays,
    carry_in,
    carry_out,
    prefix,
    start,
    part,
    top_buf,
    sum_buf,
    acc_buf,
    square_own,
    square_other,
    kv_send,
    kv_recv,
    q_send,
    q_recv,
    state_send,
    state_recv,
    decay_send,
    decay_recv,
    up_send,
    up_recv,
    chain_send,
    chain_recv,
    prefix_send,
    prefix_recv,
    o_send,
    o_recv,
    square_send,
    square_recv,
):
    rows = x_ref.shape[0]
    width = x_ref.shape[1]
    quarter = width // GROUP
    blocks = width // BLOCK
    own = lax.axis_index("ctx")
    place, level = own % GROUP, own // GROUP
    top = groups - 1
    base = level * GROUP
    peer_place = [xor_place(place, j) for j in range(GROUP)]
    other = 1 - lax.axis_index("heads")

    def remote(src, dst, send, recv, **device):
        return pltpu.make_async_remote_copy(
            src_ref=src,
            dst_ref=dst,
            send_sem=send,
            recv_sem=recv,
            device_id=device,
            device_id_type=MESH,
        )

    def to_peer(j, src, dst, send, recv):
        return remote(src, dst, send, recv, ctx=base + peer_place[j])

    key_sets = key_ref.shape[1] // GROUP
    query_sets = query_ref.shape[1] // GROUP

    def kv_copies(j):
        columns = lanes(peer_place[j] * key_sets, key_sets)
        return [
            to_peer(
                j,
                ref.at[:, columns],
                kv_buf.at[0, j, :, pl.ds(k * key_sets, key_sets)],
                kv_send.at[k, j - 1],
                kv_recv.at[k, j - 1],
            )
            for k, ref in enumerate((key_ref, value_ref))
        ]

    def q_copy(j):
        columns = lanes(peer_place[j] * query_sets, query_sets)
        return to_peer(
            j, query_ref.at[:, columns], q_buf.at[j], q_send.at[j - 1], q_recv.at[j - 1]
        )

    def state_copies(j):
        return [
            to_peer(
                j, own_states.at[j], states.at[j], state_send.at[j - 1], state_recv.at[j - 1]
            ),
            to_peer(
                j, own_decays.at[j], decays.at[j], decay_send.at[j - 1], decay_recv.at[j - 1]
            ),
        ]

    def up_copy(step, j):
        return remote(
            kv_buf.at[step, j],
            kv_buf.at[step + 1, j],
            up_send.at[step, j],
            up_recv.at[step, j],
            ctx=lax.rem(own + GROUP, groups * GROUP),
        )

    piece = quarter // CHAIN

    def chain_copy(c):
        return remote(
            carry_out.at[c],
            carry_in.at[c],
            chain_send.at[c],
            chain_recv.at[c],
            ctx=lax.rem(own + GROUP, groups * GROUP),
        )

    def prefix_copy(c, j, landing):
        return to_peer(
            j,
            prefix.at[peer_place[j], c],
            start.at[:, lanes(landing * quarter + c * piece, piece)],
            prefix_send.at[c, j - 1],
            prefix_recv.at[c, j - 1],
        )

    def o_copy(j, landing):
        return to_peer(
            j,
            o_buf.at[j],
            attn_ref.at[:, lanes(landing * query_sets, query_sets)],
            o_send.at[j - 1],
            o_recv.at[j - 1],
        )

    def square_copy():
        return remote(square_own, square_other, square_send.at[0], square_recv.at[0], heads=other)

    barrier = pltpu.get_barrier_semaphore()
    for j in range(1, GROUP):
        pl.semaphore_signal(
            barrier, inc=1, device_id={"ctx": base + peer_place[j]}, device_id_type=MESH
        )
    pl.semaphore_signal(barrier, inc=1, device_id={"heads": other}, device_id_type=MESH)

    for step in (GROUP, (groups - 1) * GROUP):
        neighbour = lax.rem(own + step, groups * GROUP)
        pl.semaphore_signal(barrier, inc=1, device_id={"ctx": neighbour}, device_id_type=MESH)
    pl.semaphore_wait(barrier, GROUP + 2)

    for j in range(1, GROUP):
        for copy in kv_copies(j):
            copy.start()
    own_columns = lanes(place * key_sets, key_sets)
    kv_buf[0, 0, :, 0:key_sets] = key_ref[:, own_columns]
    kv_buf[0, 0, :, key_sets:] = value_ref[:, own_columns]

    def state_block(j, b):
        index = peer_place[j] * (quarter // BLOCK) + b
        cum = cum_ref[index]
        last = cum[rows - 1 :, :]
        weight = expand_heads(jnp.exp(last - cum))
        scaled = (x_ref[:, lanes(index * BLOCK, BLOCK)].astype(F32) * weight).astype(BF16)
        state = lax.dot_general(
            write_ref[...], scaled, (((0,), (0,)), ((), ())), preferred_element_type=F32
        )
        decay = expand_heads(jnp.exp(jnp.broadcast_to(last, (8, WIDE))))
        columns = slice(b * BLOCK, (b + 1) * BLOCK)
        if j == 0:
            states[0, :, columns] = state.astype(BF16)
            decays[0, :, columns] = decay
        else:
            own_states[j, :, columns] = state.astype(BF16)
            own_decays[j, :, columns] = decay

    for j in (3, 1, 2, 0):
        for b in range(quarter // BLOCK):
            state_block(j, b)
        if j > 0:
            for copy in state_copies(j):
                copy.start()
    for j in range(1, GROUP):
        q_copy(j).start()
    q_buf[0] = query_ref[:, lanes(place * query_sets, query_sets)]

    def forward(step):
        if step < groups - 1:

            @pl.when((level >= step) & (level < top))
            def _():
                for j in range(GROUP):
                    if step > 0:
                        up_copy(step - 1, j).wait_recv()
                    up_copy(step, j).start()

        if step > 0:

            @pl.when((level >= step) & (level == top))
            def _():
                for j in range(GROUP):
                    up_copy(step - 1, j).wait_recv()

    inner = lax.dot_general(
        read_ref[...], write_ref[...], (((1,), (1,)), ((), ())), preferred_element_type=F32
    )
    later = lax.broadcasted_iota(jnp.int32, (rows, rows), 0)
    earlier = lax.broadcasted_iota(jnp.int32, (rows, rows), 1)
    inner = jnp.where(earlier <= later, inner, 0.0)
    left = lax.broadcasted_iota(jnp.int32, (rows, 2 * HEAD_P), 1) < HEAD_P

    def local_block(index, carry):
        cum = cum_ref[index]
        cum_t = cum_t_ref[index]
        for pair in range(WIDE // 2):
            columns = lanes(index * BLOCK + pair * 2 * HEAD_P, 2 * HEAD_P)
            x_pair = x_ref[:, columns]
            halves = []
            for h in (2 * pair, 2 * pair + 1):
                gap = cum[:, h : h + 1] - cum_t[h : h + 1, :]
                mix = (jnp.exp(jnp.minimum(gap, 0.0)) * inner).astype(BF16)
                halves.append(jnp.dot(mix, x_pair, preferred_element_type=F32))
            mixed = jnp.where(left, halves[0], halves[1])
            part[:, columns] = mixed + skip_ref[:, columns] * x_pair.astype(F32)
        return carry

    lax.fori_loop(0, blocks // 2, local_block, 0)
    for j in range(1, GROUP):
        for copy in kv_copies(j):
            copy.wait_recv()
    forward(0)
    lax.fori_loop(blocks // 2, blocks, local_block, 0)

    def chain():
        for c in range(CHAIN):
            columns = slice(c * piece, (c + 1) * piece)

            @pl.when(level > 0)
            def _():
                chain_copy(c).wait_recv()

            @pl.when(level == 0)
            def _():
                carry_in[c] = jnp.zeros(carry_in.shape[1:], BF16)

            state = carry_in[c].astype(F32)
            for k in range(GROUP):
                prefix[k, c] = state.astype(BF16)
                j = xor_place(place, k)
                state = decays[j, 0:1, columns] * state + states[j, :, columns].astype(F32)
            carry_out[c] = state.astype(BF16)

            @pl.when(level < top)
            def _():
                chain_copy(c).start()

            for j in range(1, GROUP):
                prefix_copy(c, j, place).start()
            start[:, lanes(place * quarter + c * piece, piece)] = prefix[place, c]

    factor = LOG2E / math.sqrt(HEAD_DIM)
    heads = query_sets // HEAD_DIM
    key_count = GROUP * rows

    def attend(step):
        first = step == 0
        keys = kv_buf[step, :, :, 0:HEAD_DIM].reshape(key_count, HEAD_DIM)
        values = kv_buf[step, :, :, HEAD_DIM:].reshape(key_count, HEAD_DIM)
        if first:
            column = lax.broadcasted_iota(jnp.int32, (1, key_count), 1)
            shift = place * rows
            for j in range(1, GROUP):
                shift = jnp.where(column >= j * rows, (peer_place[j] - j) * rows, shift)
            positions = column + shift

        def one(block, carry):
            if first:
                row = lax.broadcasted_iota(jnp.int32, (rows, 1), 0)
                visible = positions <= row + xor_place(place, block) * rows
            for h in range(heads):
                at = block * heads + h
                query = q_buf[block, :, h * HEAD_DIM : (h + 1) * HEAD_DIM]
                scores = lax.dot_general(
                    query, keys, (((1,), (1,)), ((), ())), preferred_element_type=F32
                )
                if first:
                    scores = jnp.where(visible, scores, -1e30)
                new_max = jnp.max(scores, axis=1, keepdims=True)
                if not first:
                    new_max = jnp.maximum(new_max, top_buf[at][:, :1])
                weights = jnp.exp2((scores - new_max) * factor)
                new_sum = weights[:, :HEAD_DIM]
                for k in range(1, key_count // HEAD_DIM):
                    new_sum = new_sum + weights[:, k * HEAD_DIM : (k + 1) * HEAD_DIM]
                new_acc = jnp.dot(weights.astype(BF16), values, preferred_element_type=F32)
                if not first:
                    rescale = jnp.exp2((top_buf[at] - new_max) * factor)
                    new_sum = new_sum + rescale * sum_buf[at]
                    new_acc = new_acc + rescale * acc_buf[at]
                top_buf[at] = jnp.broadcast_to(new_max, (rows, HEAD_DIM))
                sum_buf[at] = new_sum
                acc_buf[at] = new_acc
            return carry

        lax.fori_loop(0, GROUP, one, 0)

    for j in range(1, GROUP):
        for copy in state_copies(j):
            copy.wait_recv()
    pl.when(level == 0)(chain)
    for j in range(1, GROUP):
        q_copy(j).wait_recv()
    attend(0)
    for step in range(1, groups):
        forward(step)
        if step < groups - 1:
            pl.when(level == step)(chain)
        else:
            pl.when(level == top)(chain)
        pl.when(level >= step)(functools.partial(attend, step))

    for j in (3, 1, 2, 0):
        for h in range(heads):
            total = jnp.sum(sum_buf[j * heads + h], axis=1, keepdims=True)
            o_buf[j, :, h * HEAD_DIM : (h + 1) * HEAD_DIM] = (
                acc_buf[j * heads + h] / total
            ).astype(BF16)
        if j > 0:
            o_copy(j, place).start()
    attn_ref[:, lanes(place * query_sets, query_sets)] = o_buf[0]

    for c in range(CHAIN):
        for j in range(1, GROUP):
            prefix_copy(c, j, peer_place[j]).wait_recv()
    square_own[...] = jnp.zeros(square_own.shape, F32)

    def gate_block(index, carry):
        columns = lanes(index * BLOCK, BLOCK)
        carried = jnp.dot(read_ref[...], start[:, columns], preferred_element_type=F32)
        gate = gate_ref[:, columns].astype(F32)
        mixed = part[:, columns] + expand_heads(jnp.exp(cum_ref[index])) * carried
        gated = mixed * (gate / (1.0 + jnp.exp(-gate)))
        part[:, columns] = gated
        square = gated * gated
        total = square_own[...]
        for k in range(BLOCK // 128):
            total = total + square[:, k * 128 : (k + 1) * 128]
        square_own[...] = total
        return carry

    lax.fori_loop(0, blocks, gate_block, 0)
    square_copy().start()
    square_copy().wait_recv()
    squares = jnp.sum(square_own[...] + square_other[...], axis=1, keepdims=True)
    row_scale = lax.rsqrt(squares / (SSM_HEADS * HEAD_P) + 1e-05)

    def norm_block(index, carry):
        columns = lanes(index * BLOCK, BLOCK)
        ssm_ref[:, columns] = (part[:, columns] * row_scale * gain_ref[:, columns]).astype(BF16)
        return carry

    lax.fori_loop(0, blocks, norm_block, 0)

    square_copy().wait_send()
    for j in range(1, GROUP):
        o_copy(j, peer_place[j]).wait_recv()
        o_copy(j, place).wait_send()
        q_copy(j).wait_send()
        for copy in kv_copies(j) + state_copies(j):
            copy.wait_send()
        for c in range(CHAIN):
            prefix_copy(c, j, place).wait_send()
    for step in range(groups - 1):

        @pl.when((level >= step) & (level < top))
        def _():
            for j in range(GROUP):
                up_copy(step, j).wait_send()

    @pl.when(level < top)
    def _():
        for c in range(CHAIN):
            chain_copy(c).wait_send()


def grouped_body(
    groups,
    ssm_input,
    gate_input,
    write_proj,
    read_proj,
    log_decay,
    skip_gain,
    norm_gain,
    query_rows,
    key_rows,
    value_rows,
):
    rows, width = ssm_input.shape
    steps = width // BLOCK
    quarter = width // GROUP
    causal = (jnp.arange(rows)[:, None] >= jnp.arange(rows)[None, :]).astype(F32)
    cum = jnp.dot(causal, log_decay, precision=lax.Precision.HIGHEST)
    cum_blocks = jnp.transpose(cum.reshape(rows, steps, WIDE), (1, 0, 2))
    cum_t = cum.T.reshape(steps, WIDE, rows)
    query_sets = query_rows.shape[1] // GROUP
    pairs = 2 * key_rows.shape[1] // GROUP
    heads = query_sets // HEAD_DIM
    piece = quarter // CHAIN
    vmem = pl.BlockSpec(memory_space=pltpu.VMEM)
    dma = pltpu.SemaphoreType.DMA
    others = GROUP - 1
    return pl.pallas_call(
        functools.partial(grouped_kernel, groups),
        in_specs=[vmem] * 11,
        out_specs=[vmem] * 2,
        out_shape=[
            jax.ShapeDtypeStruct((rows, width), BF16),
            jax.ShapeDtypeStruct(query_rows.shape, BF16),
        ],
        scratch_shapes=[
            pltpu.VMEM((groups, GROUP, rows, pairs), BF16),
            pltpu.VMEM((GROUP, rows, query_sets), BF16),
            pltpu.VMEM((GROUP, rows, query_sets), BF16),
            pltpu.VMEM((GROUP, STATE, quarter), BF16),
            pltpu.VMEM((GROUP, STATE, quarter), BF16),
            pltpu.VMEM((GROUP, 8, quarter), F32),
            pltpu.VMEM((GROUP, 8, quarter), F32),
            pltpu.VMEM((CHAIN, STATE, piece), BF16),
            pltpu.VMEM((CHAIN, STATE, piece), BF16),
            pltpu.VMEM((GROUP, CHAIN, STATE, piece), BF16),
            pltpu.VMEM((STATE, width), BF16),
            pltpu.VMEM((rows, width), F32),
            pltpu.VMEM((GROUP * heads, rows, HEAD_DIM), F32),
            pltpu.VMEM((GROUP * heads, rows, HEAD_DIM), F32),
            pltpu.VMEM((GROUP * heads, rows, HEAD_DIM), F32),
            pltpu.VMEM((rows, 128), F32),
            pltpu.VMEM((rows, 128), F32),
            dma((2, others)),
            dma((2, others)),
            dma((others,)),
            dma((others,)),
            dma((others,)),
            dma((others,)),
            dma((others,)),
            dma((others,)),
            dma((groups - 1, GROUP)),
            dma((groups - 1, GROUP)),
            dma((CHAIN,)),
            dma((CHAIN,)),
            dma((CHAIN, others)),
            dma((CHAIN, others)),
            dma((others,)),
            dma((others,)),
            dma((1,)),
            dma((1,)),
        ],
        compiler_params=pltpu.CompilerParams(
            collective_id=0, has_side_effects=True, vmem_limit_bytes=50 * 2**20
        ),
        cost_estimate=pl.CostEstimate(
            flops=6 * 10**9, bytes_accessed=10 * 2**20, transcendentals=12 * 10**6
        ),
        name="hybrid_layers",
    )(
        ssm_input,
        gate_input,
        write_proj,
        read_proj,
        cum_blocks,
        cum_t,
        jnp.repeat(skip_gain, HEAD_P)[None],
        norm_gain[None],
        query_rows,
        key_rows,
        value_rows,
    )


def solution(mesh):
    in_specs = (
        P("ctx", "heads"),
        P("ctx", "heads"),
        P("ctx", None),
        P("ctx", None),
        P("ctx", "heads"),
        P("heads"),
        P("heads"),
        P("ctx", "heads"),
        P("ctx", "heads"),
        P("ctx", "heads"),
    )
    out_specs = (P("ctx", "heads"), P("ctx", "heads"))
    ctx, heads = mesh.shape["ctx"], mesh.shape["heads"]
    grouped = ctx % GROUP == 0 and ctx > GROUP and KV_HEADS // heads == GROUP and heads == 2
    chosen = functools.partial(grouped_body, ctx // GROUP) if grouped else body
    return jax.shard_map(chosen, mesh=mesh, in_specs=in_specs, out_specs=out_specs, check_vma=False)
```

```python
import functools
import math

import jax
import jax.numpy as jnp
from jax import lax
from jax.experimental import pallas as pl
from jax.experimental.pallas import tpu as pltpu
from jax.sharding import PartitionSpec as P

SSM_HEADS = 128
HEAD_P = 64
STATE = 128
QUERY_HEADS = 32
KV_HEADS = 8
HEAD_DIM = 128
SPAN = 64


def carried_in(part, axis, combine, identity):
    place = lax.axis_index(axis)
    gathered = jax.tree.map(lambda a: lax.all_gather(a, axis), part)
    state = jax.tree.map(lambda a, e: jnp.zeros_like(a) + jnp.asarray(e, a.dtype), part, identity)

    def one(step, state):
        return combine(
            state, jax.tree.map(lambda a: lax.dynamic_index_in_dim(a, step, 0, False), gathered)
        )

    return lax.fori_loop(0, place, one, state)


def chain_combine(earlier, later):
    return (earlier[0] * later[0], later[0][:, None, None] * earlier[1] + later[1])


def local_mixer(ssm_input, gate_input, write_proj, read_proj, log_decay, skip_gain, norm_gain):
    row_count, width_local = ssm_input.shape
    head_local = log_decay.shape[1]
    block_count = row_count // SPAN
    inputs_blk = ssm_input.reshape(block_count, SPAN, head_local, HEAD_P)
    inputs_float = inputs_blk.astype(jnp.float32)
    write_blk = write_proj.reshape(block_count, SPAN, STATE)
    read_blk = read_proj.reshape(block_count, SPAN, STATE)
    cum_decay = jnp.cumsum(log_decay.reshape(block_count, SPAN, head_local), axis=1)
    cum_heads = jnp.transpose(cum_decay, (0, 2, 1))
    causal = jnp.arange(SPAN)[:, None] >= jnp.arange(SPAN)[None, :]
    decay_gap = cum_heads[:, :, :, None] - cum_heads[:, :, None, :]
    decay_mask = jnp.where(causal, jnp.exp(jnp.where(causal, decay_gap, 0.0)), 0.0)
    intersection = jnp.einsum(
        "ctn,csn->cts", read_blk, write_blk, preferred_element_type=jnp.float32
    )
    mix_weights = intersection[:, None] * decay_mask
    y_local = jnp.einsum(
        "chts,cshp->cthp", mix_weights, inputs_float, precision=lax.Precision.HIGHEST
    )
    tail_decay = jnp.exp(cum_heads[:, :, -1:] - cum_heads)
    weighted_write = tail_decay[:, :, :, None] * write_blk[:, None].astype(jnp.float32)
    block_state = jnp.einsum(
        "cshp,chsn->chpn", inputs_float, weighted_write, precision=lax.Precision.HIGHEST
    )
    block_decay = jnp.exp(cum_heads[:, :, -1])

    def prefix_step(carry_in, block_item):
        return (chain_combine(carry_in, block_item), carry_in)

    start_pair = (
        jnp.ones((head_local,), jnp.float32),
        jnp.zeros((head_local, HEAD_P, STATE), jnp.float32),
    )
    device_pair, prefix_pair = lax.scan(prefix_step, start_pair, (block_decay, block_state))
    incoming = carried_in(device_pair, "ctx", chain_combine, start_pair)
    start_state = prefix_pair[0][:, :, None, None] * incoming[1][None] + prefix_pair[1]
    y_carry = (
        jnp.einsum(
            "ctn,chpn->cthp",
            read_blk.astype(jnp.float32),
            start_state,
            precision=lax.Precision.HIGHEST,
        )
        * jnp.exp(cum_decay)[:, :, :, None]
    )
    mixed_out = y_local + y_carry + skip_gain[None, None, :, None] * inputs_float
    gated = mixed_out.reshape(row_count, width_local) * jax.nn.silu(gate_input.astype(jnp.float32))
    square_total = lax.psum(jnp.sum(gated * gated, axis=1), "heads")
    row_scale = lax.rsqrt(square_total / (SSM_HEADS * HEAD_P) + 1e-05)
    return (gated * row_scale[:, None] * norm_gain[None, :]).astype(jnp.bfloat16)


def attend_block(
    state, query_block, query_positions, top_position, key_block, value_block, first_key
):
    scale_factor = 1.0 / HEAD_DIM**0.5
    key_count = key_block.shape[0]

    def compute(state_in):
        running_max, running_sum, running_acc = state_in
        scores = (
            jnp.einsum("gqd,ngd->gqn", query_block, key_block, preferred_element_type=jnp.float32)
            * scale_factor
        )
        key_positions = first_key + jnp.arange(key_count, dtype=jnp.int32)
        visible = key_positions[None, None, :] <= query_positions[None, :, None]
        block_max = jnp.max(jnp.where(visible, scores, -1e30), axis=2)
        new_max = jnp.maximum(running_max, block_max)
        weights = jnp.where(
            visible, jnp.exp(jnp.where(visible, scores - new_max[:, :, None], 0.0)), 0.0
        )
        rescale = jnp.exp(running_max - new_max)
        new_sum = rescale * running_sum + jnp.sum(weights, axis=2)
        new_acc = rescale[:, :, None] * running_acc + jnp.einsum(
            "gqn,ngd->gqd",
            weights.astype(jnp.bfloat16),
            value_block,
            preferred_element_type=jnp.float32,
        )
        return (new_max, new_sum, new_acc)

    return lax.cond(first_key > top_position, lambda state_in: state_in, compute, state)


def attention_local(query_rows, key_rows, value_rows):
    row_count = query_rows.shape[0]
    head_sets = key_rows.shape[1] // HEAD_DIM
    group_size = QUERY_HEADS // KV_HEADS
    own_index = lax.axis_index("ctx")
    query_stack = query_rows.reshape(row_count, head_sets, group_size, HEAD_DIM)
    query_stack = jnp.transpose(query_stack, (1, 0, 2, 3)).reshape(
        head_sets, row_count * group_size, HEAD_DIM
    )
    stacked_rows = jnp.arange(row_count * group_size, dtype=jnp.int32) // group_size
    own_positions = own_index * row_count + stacked_rows
    query_sets = [(query_stack, own_positions)]
    tops = [jnp.max(positions) for _, positions in query_sets]
    carries = tuple(
        (
            (
                jnp.full((head_sets, block.shape[1]), -1e30, jnp.float32),
                jnp.zeros((head_sets, block.shape[1]), jnp.float32),
                jnp.zeros((head_sets, block.shape[1], HEAD_DIM), jnp.float32),
            )
            for block, _ in query_sets
        )
    )
    key_piece = lax.all_gather(key_rows, "ctx", axis=0, tiled=True)
    value_piece = lax.all_gather(value_rows, "ctx", axis=0, tiled=True)
    piece_rows = key_piece.shape[0]
    key_blocks = key_piece.reshape(piece_rows // row_count, row_count, head_sets, HEAD_DIM)
    value_blocks = value_piece.reshape(piece_rows // row_count, row_count, head_sets, HEAD_DIM)
    offsets = row_count * jnp.arange(piece_rows // row_count, dtype=jnp.int32)

    def inner_step(states, block_item):
        key_block, value_block, first_key = block_item
        updated = tuple(
            (
                attend_block(
                    states[number],
                    query_sets[number][0],
                    query_sets[number][1],
                    tops[number],
                    key_block,
                    value_block,
                    first_key,
                )
                for number in range(len(query_sets))
            )
        )
        return (updated, None)

    result, _ = lax.scan(inner_step, carries, (key_blocks, value_blocks, offsets))
    finished = [(state[2] / state[1][:, :, None]).astype(jnp.bfloat16) for state in result]
    combined = finished[0]
    combined = combined.reshape(head_sets, row_count, group_size, HEAD_DIM)
    return jnp.transpose(combined, (1, 0, 2, 3)).reshape(
        row_count, head_sets * group_size * HEAD_DIM
    )


def body(
    ssm_input,
    gate_input,
    write_proj,
    read_proj,
    log_decay,
    skip_gain,
    norm_gain,
    query_rows,
    key_rows,
    value_rows,
):
    ssm_out = local_mixer(
        ssm_input, gate_input, write_proj, read_proj, log_decay, skip_gain, norm_gain
    )
    attn_out = attention_local(query_rows, key_rows, value_rows)
    return (ssm_out, attn_out)


GROUP = 4
WIDE = 8
BLOCK = WIDE * HEAD_P
CHAIN = 4
F32 = jnp.float32
BF16 = jnp.bfloat16
LOG2E = math.log2(math.e)
MESH = pl.DeviceIdType.MESH


def xor_place(a, b):
    a1, a0, b1, b0 = a // 2, a % 2, b // 2, b % 2
    return 2 * (a1 + b1 - 2 * a1 * b1) + (a0 + b0 - 2 * a0 * b0)


def lanes(start, size):
    return pl.ds(pl.multiple_of(start, 128), size)


def expand_heads(per_head):
    first = lax.broadcasted_iota(jnp.int32, (WIDE, BLOCK), 0) * HEAD_P
    column = lax.broadcasted_iota(jnp.int32, (WIDE, BLOCK), 1)
    spread = jnp.where((column >= first) & (column < first + HEAD_P), 1.0, 0.0).astype(BF16)
    high = per_head.astype(BF16)
    low = (per_head - high.astype(F32)).astype(BF16)
    return jnp.dot(high, spread, preferred_element_type=F32) + jnp.dot(
        low, spread, preferred_element_type=F32
    )


def grouped_kernel(
    groups,
    x_hbm,
    gate_hbm,
    write_ref,
    read_ref,
    cum_ref,
    cum_t_ref,
    skip_ref,
    gain_ref,
    query_ref,
    key_ref,
    value_ref,
    ssm_ref,
    attn_ref,
    x_ref,
    gate_ref,
    kv_buf,
    q_buf,
    o_buf,
    own_states,
    states,
    own_decays,
    decays,
    carry_in,
    carry_out,
    prefix,
    start,
    part,
    top_buf,
    sum_buf,
    acc_buf,
    square_own,
    square_other,
    load_sem,
    kv_send,
    kv_recv,
    q_send,
    q_recv,
    state_send,
    state_recv,
    decay_send,
    decay_recv,
    up_send,
    up_recv,
    chain_send,
    chain_recv,
    prefix_send,
    prefix_recv,
    o_send,
    o_recv,
    square_send,
    square_recv,
):
    rows, width = x_ref.shape
    quarter = width // GROUP
    blocks = width // BLOCK
    own = lax.axis_index("ctx")
    place, level = own % GROUP, own // GROUP
    top = groups - 1
    base = level * GROUP
    peer_place = [xor_place(place, j) for j in range(GROUP)]
    other = 1 - lax.axis_index("heads")

    def remote(src, dst, send, recv, **device):
        return pltpu.make_async_remote_copy(
            src_ref=src,
            dst_ref=dst,
            send_sem=send,
            recv_sem=recv,
            device_id=device,
            device_id_type=MESH,
        )

    def to_peer(j, src, dst, send, recv):
        return remote(src, dst, send, recv, ctx=base + peer_place[j])

    key_sets = key_ref.shape[1] // GROUP
    query_sets = query_ref.shape[1] // GROUP

    def kv_copies(j):
        columns = lanes(peer_place[j] * key_sets, key_sets)
        return [
            to_peer(
                j,
                ref.at[:, columns],
                kv_buf.at[0, j, :, pl.ds(k * key_sets, key_sets)],
                kv_send.at[k, j - 1],
                kv_recv.at[k, j - 1],
            )
            for k, ref in enumerate((key_ref, value_ref))
        ]

    def q_copy(j):
        columns = lanes(peer_place[j] * query_sets, query_sets)
        return to_peer(
            j, query_ref.at[:, columns], q_buf.at[j], q_send.at[j - 1], q_recv.at[j - 1]
        )

    def state_copies(j):
        return [
            to_peer(
                j, own_states.at[j], states.at[j], state_send.at[j - 1], state_recv.at[j - 1]
            ),
            to_peer(
                j, own_decays.at[j], decays.at[j], decay_send.at[j - 1], decay_recv.at[j - 1]
            ),
        ]

    def up_copy(step, j):
        return remote(
            kv_buf.at[step, j],
            kv_buf.at[step + 1, j],
            up_send.at[step, j],
            up_recv.at[step, j],
            ctx=lax.rem(own + GROUP, groups * GROUP),
        )

    piece = quarter // CHAIN

    def chain_copy(c):
        return remote(
            carry_out.at[c],
            carry_in.at[c],
            chain_send.at[c],
            chain_recv.at[c],
            ctx=lax.rem(own + GROUP, groups * GROUP),
        )

    def prefix_copy(c, j, landing):
        return to_peer(
            j,
            prefix.at[peer_place[j], c],
            start.at[:, lanes(landing * quarter + c * piece, piece)],
            prefix_send.at[c, j - 1],
            prefix_recv.at[c, j - 1],
        )

    def o_copy(j, landing):
        return to_peer(
            j,
            o_buf.at[j],
            attn_ref.at[:, lanes(landing * query_sets, query_sets)],
            o_send.at[j - 1],
            o_recv.at[j - 1],
        )

    def square_copy():
        return remote(square_own, square_other, square_send.at[0], square_recv.at[0], heads=other)

    def loads():
        own_keys = lanes(place * key_sets, key_sets)
        pairs = [
            (x_hbm, x_ref),
            (key_ref.at[:, own_keys], kv_buf.at[0, 0, :, pl.ds(0, key_sets)]),
            (value_ref.at[:, own_keys], kv_buf.at[0, 0, :, pl.ds(key_sets, key_sets)]),
            (query_ref.at[:, lanes(place * query_sets, query_sets)], q_buf.at[0]),
            (gate_hbm, gate_ref),
        ]
        return [
            pltpu.make_async_copy(src, dst, load_sem.at[n]) for n, (src, dst) in enumerate(pairs)
        ]

    for copy in loads():
        copy.start()

    barrier = pltpu.get_barrier_semaphore()
    for j in range(1, GROUP):
        pl.semaphore_signal(
            barrier, inc=1, device_id={"ctx": base + peer_place[j]}, device_id_type=MESH
        )
    pl.semaphore_signal(barrier, inc=1, device_id={"heads": other}, device_id_type=MESH)

    for step in (GROUP, (groups - 1) * GROUP):
        neighbour = lax.rem(own + step, groups * GROUP)
        pl.semaphore_signal(barrier, inc=1, device_id={"ctx": neighbour}, device_id_type=MESH)
    pl.semaphore_wait(barrier, GROUP + 2)

    for j in range(1, GROUP):
        for copy in kv_copies(j):
            copy.start()
    for j in range(1, GROUP):
        q_copy(j).start()
    loads()[0].wait()

    def state_block(j, b):
        index = peer_place[j] * (quarter // BLOCK) + b
        cum = cum_ref[index]
        last = cum[rows - 1 :, :]
        weight = expand_heads(jnp.exp(last - cum))
        scaled = (x_ref[:, lanes(index * BLOCK, BLOCK)].astype(F32) * weight).astype(BF16)
        state = lax.dot_general(
            write_ref[...], scaled, (((0,), (0,)), ((), ())), preferred_element_type=F32
        )
        decay = expand_heads(jnp.exp(jnp.broadcast_to(last, (8, WIDE))))
        columns = slice(b * BLOCK, (b + 1) * BLOCK)
        if j == 0:
            states[0, :, columns] = state.astype(BF16)
            decays[0, :, columns] = decay
        else:
            own_states[j, :, columns] = state.astype(BF16)
            own_decays[j, :, columns] = decay

    for j in (3, 1, 2, 0):
        for b in range(quarter // BLOCK):
            state_block(j, b)
        if j > 0:
            for copy in state_copies(j):
                copy.start()

    def forward(step):
        if step < groups - 1:

            @pl.when((level >= step) & (level < top))
            def _():
                for j in range(GROUP):
                    if step > 0:
                        up_copy(step - 1, j).wait_recv()
                    up_copy(step, j).start()

        if step > 0:

            @pl.when((level >= step) & (level == top))
            def _():
                for j in range(GROUP):
                    up_copy(step - 1, j).wait_recv()

    inner = lax.dot_general(
        read_ref[...], write_ref[...], (((1,), (1,)), ((), ())), preferred_element_type=F32
    )
    later = lax.broadcasted_iota(jnp.int32, (rows, rows), 0)
    earlier = lax.broadcasted_iota(jnp.int32, (rows, rows), 1)
    inner = jnp.where(earlier <= later, inner, 0.0)
    left = lax.broadcasted_iota(jnp.int32, (rows, 2 * HEAD_P), 1) < HEAD_P

    def local_block(index, carry):
        cum = cum_ref[index]
        cum_t = cum_t_ref[index]
        for pair in range(WIDE // 2):
            columns = lanes(index * BLOCK + pair * 2 * HEAD_P, 2 * HEAD_P)
            x_pair = x_ref[:, columns]
            halves = []
            for h in (2 * pair, 2 * pair + 1):
                gap = cum[:, h : h + 1] - cum_t[h : h + 1, :]
                mix = (jnp.exp(jnp.minimum(gap, 0.0)) * inner).astype(BF16)
                halves.append(jnp.dot(mix, x_pair, preferred_element_type=F32))
            mixed = jnp.where(left, halves[0], halves[1])
            part[:, columns] = mixed + skip_ref[:, columns] * x_pair.astype(F32)
        return carry

    lax.fori_loop(0, blocks // 2, local_block, 0)
    for copy in loads()[1:]:
        copy.wait()
    for j in range(1, GROUP):
        for copy in kv_copies(j):
            copy.wait_recv()
    forward(0)
    lax.fori_loop(blocks // 2, blocks, local_block, 0)

    def chain():
        for c in range(CHAIN):
            columns = slice(c * piece, (c + 1) * piece)

            @pl.when(level > 0)
            def _():
                chain_copy(c).wait_recv()

            @pl.when(level == 0)
            def _():
                carry_in[c] = jnp.zeros(carry_in.shape[1:], BF16)

            state = carry_in[c].astype(F32)
            for k in range(GROUP):
                prefix[k, c] = state.astype(BF16)
                j = xor_place(place, k)
                state = decays[j, 0:1, columns] * state + states[j, :, columns].astype(F32)
            carry_out[c] = state.astype(BF16)

            @pl.when(level < top)
            def _():
                chain_copy(c).start()

            for j in range(1, GROUP):
                prefix_copy(c, j, place).start()
            start[:, lanes(place * quarter + c * piece, piece)] = prefix[place, c]

    factor = LOG2E / math.sqrt(HEAD_DIM)
    heads = query_sets // HEAD_DIM
    key_count = GROUP * rows

    def own_blocks(count):
        keys_values = [kv_buf[0, xor_place(place, k)] for k in range(count)]
        return jnp.concatenate(keys_values) if count > 1 else keys_values[0]

    def attend_own():
        row = lax.broadcasted_iota(jnp.int32, (rows, 1), 0)
        for block in range(GROUP):
            entry = xor_place(place, block)
            keys_values = own_blocks(block + 1)
            keys, values = keys_values[:, :HEAD_DIM], keys_values[:, HEAD_DIM:]
            key_total = (block + 1) * rows
            visible = (
                lax.broadcasted_iota(jnp.int32, (rows, key_total), 1) <= row + block * rows
            )
            for h in range(heads):
                query = q_buf[entry, :, h * HEAD_DIM : (h + 1) * HEAD_DIM]
                scores = lax.dot_general(
                    query, keys, (((1,), (1,)), ((), ())), preferred_element_type=F32
                )
                scores = jnp.where(visible, scores, -1e30)
                new_max = jnp.max(scores, axis=1, keepdims=True)
                weights = jnp.exp2((scores - new_max) * factor)
                total = jnp.sum(weights, axis=1, keepdims=True)
                lane = lax.broadcasted_iota(jnp.int32, (rows, HEAD_DIM), 1)
                at = entry * heads + h
                top_buf[at] = jnp.broadcast_to(new_max, (rows, HEAD_DIM))
                sum_buf[at] = jnp.where(lane == 0, total, 0.0)
                acc_buf[at] = jnp.dot(weights.astype(BF16), values, preferred_element_type=F32)

    def attend(step):
        keys = kv_buf[step, :, :, 0:HEAD_DIM].reshape(key_count, HEAD_DIM)
        values = kv_buf[step, :, :, HEAD_DIM:].reshape(key_count, HEAD_DIM)

        def one(block, carry):
            for h in range(heads):
                at = block * heads + h
                query = q_buf[block, :, h * HEAD_DIM : (h + 1) * HEAD_DIM]
                scores = lax.dot_general(
                    query, keys, (((1,), (1,)), ((), ())), preferred_element_type=F32
                )
                new_max = jnp.max(scores, axis=1, keepdims=True)
                new_max = jnp.maximum(new_max, top_buf[at][:, :1])
                weights = jnp.exp2((scores - new_max) * factor)
                new_sum = weights[:, :HEAD_DIM]
                for k in range(1, key_count // HEAD_DIM):
                    new_sum = new_sum + weights[:, k * HEAD_DIM : (k + 1) * HEAD_DIM]
                new_acc = jnp.dot(weights.astype(BF16), values, preferred_element_type=F32)
                rescale = jnp.exp2((top_buf[at] - new_max) * factor)
                sum_buf[at] = new_sum + rescale * sum_buf[at]
                acc_buf[at] = new_acc + rescale * acc_buf[at]
                top_buf[at] = jnp.broadcast_to(new_max, (rows, HEAD_DIM))
            return carry

        lax.fori_loop(0, GROUP, one, 0)

    for j in range(1, GROUP):
        q_copy(j).wait_recv()
    attend_own()
    for j in range(1, GROUP):
        for copy in state_copies(j):
            copy.wait_recv()
    pl.when(level == 0)(chain)
    for step in range(1, groups):
        forward(step)
        if step < groups - 1:
            pl.when(level == step)(chain)
        else:
            pl.when(level == top)(chain)
        pl.when(level >= step)(functools.partial(attend, step))

    for j in (3, 1, 2, 0):
        for h in range(heads):
            total = jnp.sum(sum_buf[j * heads + h], axis=1, keepdims=True)
            o_buf[j, :, h * HEAD_DIM : (h + 1) * HEAD_DIM] = (
                acc_buf[j * heads + h] / total
            ).astype(BF16)
        if j > 0:
            o_copy(j, place).start()
    attn_ref[:, lanes(place * query_sets, query_sets)] = o_buf[0]

    for c in range(CHAIN):
        for j in range(1, GROUP):
            prefix_copy(c, j, peer_place[j]).wait_recv()
    square_own[...] = jnp.zeros(square_own.shape, F32)

    def gate_block(index, carry):
        columns = lanes(index * BLOCK, BLOCK)
        carried = jnp.dot(read_ref[...], start[:, columns], preferred_element_type=F32)
        gate = gate_ref[:, columns].astype(F32)
        mixed = part[:, columns] + expand_heads(jnp.exp(cum_ref[index])) * carried
        gated = mixed * (gate / (1.0 + jnp.exp(-gate)))
        part[:, columns] = gated
        square = gated * gated
        total = square_own[...]
        for k in range(BLOCK // 128):
            total = total + square[:, k * 128 : (k + 1) * 128]
        square_own[...] = total
        return carry

    lax.fori_loop(0, blocks, gate_block, 0)
    square_copy().start()
    square_copy().wait_recv()
    squares = jnp.sum(square_own[...] + square_other[...], axis=1, keepdims=True)
    row_scale = lax.rsqrt(squares / (SSM_HEADS * HEAD_P) + 1e-05)

    def norm_block(index, carry):
        columns = lanes(index * BLOCK, BLOCK)
        ssm_ref[:, columns] = (part[:, columns] * row_scale * gain_ref[:, columns]).astype(BF16)
        return carry

    lax.fori_loop(0, blocks, norm_block, 0)

    square_copy().wait_send()
    for j in range(1, GROUP):
        o_copy(j, peer_place[j]).wait_recv()
        o_copy(j, place).wait_send()
        q_copy(j).wait_send()
        for copy in kv_copies(j) + state_copies(j):
            copy.wait_send()
        for c in range(CHAIN):
            prefix_copy(c, j, place).wait_send()
    for step in range(groups - 1):

        @pl.when((level >= step) & (level < top))
        def _():
            for j in range(GROUP):
                up_copy(step, j).wait_send()

    @pl.when(level < top)
    def _():
        for c in range(CHAIN):
            chain_copy(c).wait_send()


def grouped_body(
    groups,
    ssm_input,
    gate_input,
    write_proj,
    read_proj,
    log_decay,
    skip_gain,
    norm_gain,
    query_rows,
    key_rows,
    value_rows,
):
    rows, width = ssm_input.shape
    steps = width // BLOCK
    quarter = width // GROUP
    causal = (jnp.arange(rows)[:, None] >= jnp.arange(rows)[None, :]).astype(F32)
    cum = jnp.dot(causal, log_decay, precision=lax.Precision.HIGHEST)
    cum_blocks = jnp.transpose(cum.reshape(rows, steps, WIDE), (1, 0, 2))
    cum_t = cum.T.reshape(steps, WIDE, rows)
    query_sets = query_rows.shape[1] // GROUP
    pairs = 2 * key_rows.shape[1] // GROUP
    heads = query_sets // HEAD_DIM
    piece = quarter // CHAIN
    vmem = pl.BlockSpec(memory_space=pltpu.VMEM)
    hbm = pl.BlockSpec(memory_space=pl.ANY)
    dma = pltpu.SemaphoreType.DMA
    others = GROUP - 1
    return pl.pallas_call(
        functools.partial(grouped_kernel, groups),
        in_specs=[hbm] * 2 + [vmem] * 6 + [hbm] * 3,
        out_specs=[vmem] * 2,
        out_shape=[
            jax.ShapeDtypeStruct((rows, width), BF16),
            jax.ShapeDtypeStruct(query_rows.shape, BF16),
        ],
        scratch_shapes=[
            pltpu.VMEM((rows, width), BF16),
            pltpu.VMEM((rows, width), BF16),
            pltpu.VMEM((groups, GROUP, rows, pairs), BF16),
            pltpu.VMEM((GROUP, rows, query_sets), BF16),
            pltpu.VMEM((GROUP, rows, query_sets), BF16),
            pltpu.VMEM((GROUP, STATE, quarter), BF16),
            pltpu.VMEM((GROUP, STATE, quarter), BF16),
            pltpu.VMEM((GROUP, 8, quarter), F32),
            pltpu.VMEM((GROUP, 8, quarter), F32),
            pltpu.VMEM((CHAIN, STATE, piece), BF16),
            pltpu.VMEM((CHAIN, STATE, piece), BF16),
            pltpu.VMEM((GROUP, CHAIN, STATE, piece), BF16),
            pltpu.VMEM((STATE, width), BF16),
            pltpu.VMEM((rows, width), F32),
            pltpu.VMEM((GROUP * heads, rows, HEAD_DIM), F32),
            pltpu.VMEM((GROUP * heads, rows, HEAD_DIM), F32),
            pltpu.VMEM((GROUP * heads, rows, HEAD_DIM), F32),
            pltpu.VMEM((rows, 128), F32),
            pltpu.VMEM((rows, 128), F32),
            dma((5,)),
            dma((2, others)),
            dma((2, others)),
            dma((others,)),
            dma((others,)),
            dma((others,)),
            dma((others,)),
            dma((others,)),
            dma((others,)),
            dma((groups - 1, GROUP)),
            dma((groups - 1, GROUP)),
            dma((CHAIN,)),
            dma((CHAIN,)),
            dma((CHAIN, others)),
            dma((CHAIN, others)),
            dma((others,)),
            dma((others,)),
            dma((1,)),
            dma((1,)),
        ],
        compiler_params=pltpu.CompilerParams(
            collective_id=0, has_side_effects=True, vmem_limit_bytes=50 * 2**20
        ),
        cost_estimate=pl.CostEstimate(
            flops=6 * 10**9, bytes_accessed=10 * 2**20, transcendentals=12 * 10**6
        ),
        name="hybrid_layers",
    )(
        ssm_input,
        gate_input,
        write_proj,
        read_proj,
        cum_blocks,
        cum_t,
        jnp.repeat(skip_gain, HEAD_P)[None],
        norm_gain[None],
        query_rows,
        key_rows,
        value_rows,
    )


def solution(mesh):
    in_specs = (
        P("ctx", "heads"),
        P("ctx", "heads"),
        P("ctx", None),
        P("ctx", None),
        P("ctx", "heads"),
        P("heads"),
        P("heads"),
        P("ctx", "heads"),
        P("ctx", "heads"),
        P("ctx", "heads"),
    )
    out_specs = (P("ctx", "heads"), P("ctx", "heads"))
    ctx, heads = mesh.shape["ctx"], mesh.shape["heads"]
    grouped = ctx % GROUP == 0 and ctx > GROUP and KV_HEADS // heads == GROUP and heads == 2
    chosen = functools.partial(grouped_body, ctx // GROUP) if grouped else body
    return jax.shard_map(chosen, mesh=mesh, in_specs=in_specs, out_specs=out_specs, check_vma=False)
```

```python
import functools
import math

import jax
import jax.numpy as jnp
from jax import lax
from jax.experimental import pallas as pl
from jax.experimental.pallas import tpu as pltpu
from jax.sharding import PartitionSpec as P

SSM_HEADS = 128
HEAD_P = 64
STATE = 128
QUERY_HEADS = 32
KV_HEADS = 8
HEAD_DIM = 128
SPAN = 64


def carried_in(part, axis, combine, identity):
    place = lax.axis_index(axis)
    gathered = jax.tree.map(lambda a: lax.all_gather(a, axis), part)
    state = jax.tree.map(lambda a, e: jnp.zeros_like(a) + jnp.asarray(e, a.dtype), part, identity)

    def one(step, state):
        return combine(
            state, jax.tree.map(lambda a: lax.dynamic_index_in_dim(a, step, 0, False), gathered)
        )

    return lax.fori_loop(0, place, one, state)


def chain_combine(earlier, later):
    return (earlier[0] * later[0], later[0][:, None, None] * earlier[1] + later[1])


def local_mixer(ssm_input, gate_input, write_proj, read_proj, log_decay, skip_gain, norm_gain):
    row_count, width_local = ssm_input.shape
    head_local = log_decay.shape[1]
    block_count = row_count // SPAN
    inputs_blk = ssm_input.reshape(block_count, SPAN, head_local, HEAD_P)
    inputs_float = inputs_blk.astype(jnp.float32)
    write_blk = write_proj.reshape(block_count, SPAN, STATE)
    read_blk = read_proj.reshape(block_count, SPAN, STATE)
    cum_decay = jnp.cumsum(log_decay.reshape(block_count, SPAN, head_local), axis=1)
    cum_heads = jnp.transpose(cum_decay, (0, 2, 1))
    causal = jnp.arange(SPAN)[:, None] >= jnp.arange(SPAN)[None, :]
    decay_gap = cum_heads[:, :, :, None] - cum_heads[:, :, None, :]
    decay_mask = jnp.where(causal, jnp.exp(jnp.where(causal, decay_gap, 0.0)), 0.0)
    intersection = jnp.einsum(
        "ctn,csn->cts", read_blk, write_blk, preferred_element_type=jnp.float32
    )
    mix_weights = intersection[:, None] * decay_mask
    y_local = jnp.einsum(
        "chts,cshp->cthp", mix_weights, inputs_float, precision=lax.Precision.HIGHEST
    )
    tail_decay = jnp.exp(cum_heads[:, :, -1:] - cum_heads)
    weighted_write = tail_decay[:, :, :, None] * write_blk[:, None].astype(jnp.float32)
    block_state = jnp.einsum(
        "cshp,chsn->chpn", inputs_float, weighted_write, precision=lax.Precision.HIGHEST
    )
    block_decay = jnp.exp(cum_heads[:, :, -1])

    def prefix_step(carry_in, block_item):
        return (chain_combine(carry_in, block_item), carry_in)

    start_pair = (
        jnp.ones((head_local,), jnp.float32),
        jnp.zeros((head_local, HEAD_P, STATE), jnp.float32),
    )
    device_pair, prefix_pair = lax.scan(prefix_step, start_pair, (block_decay, block_state))
    incoming = carried_in(device_pair, "ctx", chain_combine, start_pair)
    start_state = prefix_pair[0][:, :, None, None] * incoming[1][None] + prefix_pair[1]
    y_carry = (
        jnp.einsum(
            "ctn,chpn->cthp",
            read_blk.astype(jnp.float32),
            start_state,
            precision=lax.Precision.HIGHEST,
        )
        * jnp.exp(cum_decay)[:, :, :, None]
    )
    mixed_out = y_local + y_carry + skip_gain[None, None, :, None] * inputs_float
    gated = mixed_out.reshape(row_count, width_local) * jax.nn.silu(gate_input.astype(jnp.float32))
    square_total = lax.psum(jnp.sum(gated * gated, axis=1), "heads")
    row_scale = lax.rsqrt(square_total / (SSM_HEADS * HEAD_P) + 1e-05)
    return (gated * row_scale[:, None] * norm_gain[None, :]).astype(jnp.bfloat16)


def attend_block(
    state, query_block, query_positions, top_position, key_block, value_block, first_key
):
    scale_factor = 1.0 / HEAD_DIM**0.5
    key_count = key_block.shape[0]

    def compute(state_in):
        running_max, running_sum, running_acc = state_in
        scores = (
            jnp.einsum("gqd,ngd->gqn", query_block, key_block, preferred_element_type=jnp.float32)
            * scale_factor
        )
        key_positions = first_key + jnp.arange(key_count, dtype=jnp.int32)
        visible = key_positions[None, None, :] <= query_positions[None, :, None]
        block_max = jnp.max(jnp.where(visible, scores, -1e30), axis=2)
        new_max = jnp.maximum(running_max, block_max)
        weights = jnp.where(
            visible, jnp.exp(jnp.where(visible, scores - new_max[:, :, None], 0.0)), 0.0
        )
        rescale = jnp.exp(running_max - new_max)
        new_sum = rescale * running_sum + jnp.sum(weights, axis=2)
        new_acc = rescale[:, :, None] * running_acc + jnp.einsum(
            "gqn,ngd->gqd",
            weights.astype(jnp.bfloat16),
            value_block,
            preferred_element_type=jnp.float32,
        )
        return (new_max, new_sum, new_acc)

    return lax.cond(first_key > top_position, lambda state_in: state_in, compute, state)


def attention_local(query_rows, key_rows, value_rows):
    row_count = query_rows.shape[0]
    head_sets = key_rows.shape[1] // HEAD_DIM
    group_size = QUERY_HEADS // KV_HEADS
    own_index = lax.axis_index("ctx")
    query_stack = query_rows.reshape(row_count, head_sets, group_size, HEAD_DIM)
    query_stack = jnp.transpose(query_stack, (1, 0, 2, 3)).reshape(
        head_sets, row_count * group_size, HEAD_DIM
    )
    stacked_rows = jnp.arange(row_count * group_size, dtype=jnp.int32) // group_size
    own_positions = own_index * row_count + stacked_rows
    query_sets = [(query_stack, own_positions)]
    tops = [jnp.max(positions) for _, positions in query_sets]
    carries = tuple(
        (
            (
                jnp.full((head_sets, block.shape[1]), -1e30, jnp.float32),
                jnp.zeros((head_sets, block.shape[1]), jnp.float32),
                jnp.zeros((head_sets, block.shape[1], HEAD_DIM), jnp.float32),
            )
            for block, _ in query_sets
        )
    )
    key_piece = lax.all_gather(key_rows, "ctx", axis=0, tiled=True)
    value_piece = lax.all_gather(value_rows, "ctx", axis=0, tiled=True)
    piece_rows = key_piece.shape[0]
    key_blocks = key_piece.reshape(piece_rows // row_count, row_count, head_sets, HEAD_DIM)
    value_blocks = value_piece.reshape(piece_rows // row_count, row_count, head_sets, HEAD_DIM)
    offsets = row_count * jnp.arange(piece_rows // row_count, dtype=jnp.int32)

    def inner_step(states, block_item):
        key_block, value_block, first_key = block_item
        updated = tuple(
            (
                attend_block(
                    states[number],
                    query_sets[number][0],
                    query_sets[number][1],
                    tops[number],
                    key_block,
                    value_block,
                    first_key,
                )
                for number in range(len(query_sets))
            )
        )
        return (updated, None)

    result, _ = lax.scan(inner_step, carries, (key_blocks, value_blocks, offsets))
    finished = [(state[2] / state[1][:, :, None]).astype(jnp.bfloat16) for state in result]
    combined = finished[0]
    combined = combined.reshape(head_sets, row_count, group_size, HEAD_DIM)
    return jnp.transpose(combined, (1, 0, 2, 3)).reshape(
        row_count, head_sets * group_size * HEAD_DIM
    )


def body(
    ssm_input,
    gate_input,
    write_proj,
    read_proj,
    log_decay,
    skip_gain,
    norm_gain,
    query_rows,
    key_rows,
    value_rows,
):
    ssm_out = local_mixer(
        ssm_input, gate_input, write_proj, read_proj, log_decay, skip_gain, norm_gain
    )
    attn_out = attention_local(query_rows, key_rows, value_rows)
    return (ssm_out, attn_out)


GROUP = 4
WIDE = 8
BLOCK = WIDE * HEAD_P
CHAIN = 4
F32 = jnp.float32
BF16 = jnp.bfloat16
LOG2E = math.log2(math.e)
MESH = pl.DeviceIdType.MESH


def xor_place(a, b):
    a1, a0, b1, b0 = a // 2, a % 2, b // 2, b % 2
    return 2 * (a1 + b1 - 2 * a1 * b1) + (a0 + b0 - 2 * a0 * b0)


def lanes(start, size):
    return pl.ds(pl.multiple_of(start, 128), size)


def spread_heads(per_head):
    first = lax.broadcasted_iota(jnp.int32, (WIDE, BLOCK), 0) * HEAD_P
    column = lax.broadcasted_iota(jnp.int32, (WIDE, BLOCK), 1)
    spread = jnp.where((column >= first) & (column < first + HEAD_P), 1.0, 0.0).astype(BF16)
    return jnp.dot(per_head.astype(BF16), spread, preferred_element_type=F32)


def expand_heads(per_head):
    high = per_head.astype(BF16)
    return spread_heads(high) + spread_heads(per_head - high.astype(F32))


def grouped_kernel(
    groups,
    x_hbm,
    gate_hbm,
    write_hbm,
    read_hbm,
    cum_hbm,
    cum_t_hbm,
    skip_hbm,
    gain_hbm,
    query_ref,
    key_ref,
    value_ref,
    ssm_ref,
    attn_ref,
    x_ref,
    gate_ref,
    write_ref,
    read_ref,
    cum_ref,
    cum_t_ref,
    skip_ref,
    gain_ref,
    kv_buf,
    q_buf,
    o_buf,
    own_states,
    states,
    own_decays,
    decays,
    carry_in,
    carry_out,
    prefix,
    start,
    part,
    top_buf,
    sum_buf,
    acc_buf,
    square_own,
    square_other,
    load_sem,
    kv_send,
    kv_recv,
    q_send,
    q_recv,
    state_send,
    state_recv,
    decay_send,
    decay_recv,
    up_send,
    up_recv,
    chain_send,
    chain_recv,
    prefix_send,
    prefix_recv,
    o_send,
    o_recv,
    square_send,
    square_recv,
):
    rows, width = x_ref.shape
    quarter = width // GROUP
    blocks = width // BLOCK
    own = lax.axis_index("ctx")
    place, level = own % GROUP, own // GROUP
    top = groups - 1
    base = level * GROUP
    peer_place = [xor_place(place, j) for j in range(GROUP)]
    other = 1 - lax.axis_index("heads")

    def remote(src, dst, send, recv, **device):
        return pltpu.make_async_remote_copy(
            src_ref=src,
            dst_ref=dst,
            send_sem=send,
            recv_sem=recv,
            device_id=device,
            device_id_type=MESH,
        )

    def to_peer(j, src, dst, send, recv):
        return remote(src, dst, send, recv, ctx=base + peer_place[j])

    key_sets = key_ref.shape[1] // GROUP
    query_sets = query_ref.shape[1] // GROUP

    def kv_copies(j):
        columns = lanes(peer_place[j] * key_sets, key_sets)
        return [
            to_peer(
                j,
                ref.at[:, columns],
                kv_buf.at[0, j, :, pl.ds(k * key_sets, key_sets)],
                kv_send.at[k, j - 1],
                kv_recv.at[k, j - 1],
            )
            for k, ref in enumerate((key_ref, value_ref))
        ]

    def q_copy(j):
        columns = lanes(peer_place[j] * query_sets, query_sets)
        return to_peer(
            j, query_ref.at[:, columns], q_buf.at[j], q_send.at[j - 1], q_recv.at[j - 1]
        )

    def state_copies(j):
        return [
            to_peer(
                j, own_states.at[j], states.at[j], state_send.at[j - 1], state_recv.at[j - 1]
            ),
            to_peer(
                j, own_decays.at[j], decays.at[j], decay_send.at[j - 1], decay_recv.at[j - 1]
            ),
        ]

    def up_copy(step, j):
        return remote(
            kv_buf.at[step, j],
            kv_buf.at[step + 1, j],
            up_send.at[step, j],
            up_recv.at[step, j],
            ctx=lax.rem(own + GROUP, groups * GROUP),
        )

    piece = quarter // CHAIN

    def chain_copy(c):
        return remote(
            carry_out.at[c],
            carry_in.at[c],
            chain_send.at[c],
            chain_recv.at[c],
            ctx=lax.rem(own + GROUP, groups * GROUP),
        )

    def prefix_copy(c, j, landing):
        return to_peer(
            j,
            prefix.at[peer_place[j], c],
            start.at[:, lanes(landing * quarter + c * piece, piece)],
            prefix_send.at[c, j - 1],
            prefix_recv.at[c, j - 1],
        )

    def o_copy(j, landing):
        return to_peer(
            j,
            o_buf.at[j],
            attn_ref.at[:, lanes(landing * query_sets, query_sets)],
            o_send.at[j - 1],
            o_recv.at[j - 1],
        )

    def square_copy():
        return remote(square_own, square_other, square_send.at[0], square_recv.at[0], heads=other)

    def loads():
        own_keys = lanes(place * key_sets, key_sets)
        pairs = [
            (x_hbm, x_ref),
            (cum_hbm, cum_ref),
            (write_hbm, write_ref),
            (read_hbm, read_ref),
            (cum_t_hbm, cum_t_ref),
            (skip_hbm, skip_ref),
            (gain_hbm, gain_ref),
            (key_ref.at[:, own_keys], kv_buf.at[0, 0, :, pl.ds(0, key_sets)]),
            (value_ref.at[:, own_keys], kv_buf.at[0, 0, :, pl.ds(key_sets, key_sets)]),
            (query_ref.at[:, lanes(place * query_sets, query_sets)], q_buf.at[0]),
            (gate_hbm, gate_ref),
        ]
        return [
            pltpu.make_async_copy(src, dst, load_sem.at[n]) for n, (src, dst) in enumerate(pairs)
        ]

    for copy in loads():
        copy.start()

    barrier = pltpu.get_barrier_semaphore()
    for j in range(1, GROUP):
        pl.semaphore_signal(
            barrier, inc=1, device_id={"ctx": base + peer_place[j]}, device_id_type=MESH
        )
    pl.semaphore_signal(barrier, inc=1, device_id={"heads": other}, device_id_type=MESH)

    for step in (GROUP, (groups - 1) * GROUP):
        neighbour = lax.rem(own + step, groups * GROUP)
        pl.semaphore_signal(barrier, inc=1, device_id={"ctx": neighbour}, device_id_type=MESH)
    pl.semaphore_wait(barrier, GROUP + 2)

    for j in range(1, GROUP):
        for copy in kv_copies(j):
            copy.start()
    for j in range(1, GROUP):
        q_copy(j).start()
    for copy in loads()[:3]:
        copy.wait()

    def state_block(j, b):
        index = peer_place[j] * (quarter // BLOCK) + b
        cum = cum_ref[index]
        last = cum[rows - 1 :, :]
        weight = spread_heads(jnp.exp(last - cum)).astype(BF16)
        scaled = x_ref[:, lanes(index * BLOCK, BLOCK)] * weight
        state = lax.dot_general(
            write_ref[...], scaled, (((0,), (0,)), ((), ())), preferred_element_type=F32
        )
        columns = slice(b * BLOCK, (b + 1) * BLOCK)
        if j == 0:
            states[0, :, columns] = state.astype(BF16)
            decays[0, b : b + 1, 0:WIDE] = last
        else:
            own_states[j, :, columns] = state.astype(BF16)
            own_decays[j, b : b + 1, 0:WIDE] = last

    own_decays[...] = jnp.zeros(own_decays.shape, F32)
    for j in (3, 1, 2, 0):
        for b in range(quarter // BLOCK):
            state_block(j, b)
        if j > 0:
            for copy in state_copies(j):
                copy.start()

    def forward(step):
        if step < groups - 1:

            @pl.when((level >= step) & (level < top))
            def _():
                for j in range(GROUP):
                    if step > 0:
                        up_copy(step - 1, j).wait_recv()
                    up_copy(step, j).start()

        if step > 0:

            @pl.when((level >= step) & (level == top))
            def _():
                for j in range(GROUP):
                    up_copy(step - 1, j).wait_recv()

    for copy in loads()[3:]:
        copy.wait()

    inner = lax.dot_general(
        read_ref[...], write_ref[...], (((1,), (1,)), ((), ())), preferred_element_type=F32
    )
    later = lax.broadcasted_iota(jnp.int32, (rows, rows), 0)
    earlier = lax.broadcasted_iota(jnp.int32, (rows, rows), 1)
    inner = jnp.where(earlier <= later, inner, 0.0)
    left = lax.broadcasted_iota(jnp.int32, (rows, 2 * HEAD_P), 1) < HEAD_P

    def local_block(index, carry):
        cum = cum_ref[index]
        cum_t = cum_t_ref[index]
        for pair in range(WIDE // 2):
            columns = lanes(index * BLOCK + pair * 2 * HEAD_P, 2 * HEAD_P)
            x_pair = x_ref[:, columns]
            halves = []
            for h in (2 * pair, 2 * pair + 1):
                gap = cum[:, h : h + 1] - cum_t[h : h + 1, :]
                mix = (jnp.exp(jnp.minimum(gap, 0.0)) * inner).astype(BF16)
                halves.append(jnp.dot(mix, x_pair, preferred_element_type=F32))
            mixed = jnp.where(left, halves[0], halves[1])
            part[:, columns] = mixed + skip_ref[:, columns] * x_pair.astype(F32)
        return carry

    lax.fori_loop(0, blocks // 2, local_block, 0)
    for j in range(1, GROUP):
        for copy in kv_copies(j):
            copy.wait_recv()
    forward(0)
    lax.fori_loop(blocks // 2, blocks, local_block, 0)

    def chain():
        for j in range(1, GROUP):
            for copy in state_copies(j):
                copy.wait_recv()
        passed = [
            [
                expand_heads(
                    jnp.exp(
                        jnp.broadcast_to(
                            decays[xor_place(place, k), b : b + 1, 0:WIDE], (8, WIDE)
                        )
                    )
                )[0:1, :]
                for b in range(quarter // BLOCK)
            ]
            for k in range(GROUP)
        ]
        for c in range(CHAIN):
            columns = slice(c * piece, (c + 1) * piece)

            @pl.when(level > 0)
            def _():
                chain_copy(c).wait_recv()

            @pl.when(level == 0)
            def _():
                carry_in[c] = jnp.zeros(carry_in.shape[1:], BF16)

            state = carry_in[c].astype(F32)
            for k in range(GROUP):
                prefix[k, c] = state.astype(BF16)
                j = xor_place(place, k)
                at = c * piece % BLOCK
                decay = passed[k][c * piece // BLOCK][:, at : at + piece]
                state = decay * state + states[j, :, columns].astype(F32)
            carry_out[c] = state.astype(BF16)

            @pl.when(level < top)
            def _():
                chain_copy(c).start()

            for j in range(1, GROUP):
                prefix_copy(c, j, place).start()
            start[:, lanes(place * quarter + c * piece, piece)] = prefix[place, c]

    factor = LOG2E / math.sqrt(HEAD_DIM)
    heads = query_sets // HEAD_DIM
    key_count = GROUP * rows

    def own_blocks(count):
        keys_values = [kv_buf[0, xor_place(place, k)] for k in range(count)]
        return jnp.concatenate(keys_values) if count > 1 else keys_values[0]

    def attend_own():
        row = lax.broadcasted_iota(jnp.int32, (rows, 1), 0)
        for block in range(GROUP):
            entry = xor_place(place, block)
            keys_values = own_blocks(block + 1)
            keys, values = keys_values[:, :HEAD_DIM], keys_values[:, HEAD_DIM:]
            key_total = (block + 1) * rows
            visible = (
                lax.broadcasted_iota(jnp.int32, (rows, key_total), 1) <= row + block * rows
            )
            for h in range(heads):
                query = q_buf[entry, :, h * HEAD_DIM : (h + 1) * HEAD_DIM]
                scores = lax.dot_general(
                    query, keys, (((1,), (1,)), ((), ())), preferred_element_type=F32
                )
                scores = jnp.where(visible, scores, -1e30)
                new_max = jnp.max(scores, axis=1, keepdims=True)
                weights = jnp.exp2((scores - new_max) * factor)
                total = jnp.sum(weights, axis=1, keepdims=True)
                lane = lax.broadcasted_iota(jnp.int32, (rows, HEAD_DIM), 1)
                at = entry * heads + h
                top_buf[at] = jnp.broadcast_to(new_max, (rows, HEAD_DIM))
                sum_buf[at] = jnp.where(lane == 0, total, 0.0)
                acc_buf[at] = jnp.dot(weights.astype(BF16), values, preferred_element_type=F32)

    def attend(step):
        keys = kv_buf[step, :, :, 0:HEAD_DIM].reshape(key_count, HEAD_DIM)
        values = kv_buf[step, :, :, HEAD_DIM:].reshape(key_count, HEAD_DIM)

        def one(block, carry):
            query = jnp.concatenate(
                [q_buf[block, :, h * HEAD_DIM : (h + 1) * HEAD_DIM] for h in range(heads)]
            )
            at = pl.ds(block * heads, heads)
            stacked = (heads * rows, HEAD_DIM)
            old_max = top_buf[at].reshape(stacked)
            scores = lax.dot_general(
                query, keys, (((1,), (1,)), ((), ())), preferred_element_type=F32
            )
            new_max = jnp.maximum(jnp.max(scores, axis=1, keepdims=True), old_max[:, :1])
            weights = jnp.exp2((scores - new_max) * factor)
            new_sum = weights[:, :HEAD_DIM]
            for k in range(1, key_count // HEAD_DIM):
                new_sum = new_sum + weights[:, k * HEAD_DIM : (k + 1) * HEAD_DIM]
            new_acc = jnp.dot(weights.astype(BF16), values, preferred_element_type=F32)
            rescale = jnp.exp2((old_max - new_max) * factor)
            new_sum = new_sum + rescale * sum_buf[at].reshape(stacked)
            new_acc = new_acc + rescale * acc_buf[at].reshape(stacked)
            shape = (heads, rows, HEAD_DIM)
            top_buf[at] = jnp.broadcast_to(new_max, stacked).reshape(shape)
            sum_buf[at] = new_sum.reshape(shape)
            acc_buf[at] = new_acc.reshape(shape)
            return carry

        lax.fori_loop(0, GROUP, one, 0)

    for j in range(1, GROUP):
        q_copy(j).wait_recv()
    attend_own()
    pl.when(level == 0)(chain)
    for step in range(1, groups):
        forward(step)
        if step < groups - 1:
            pl.when(level == step)(chain)
        else:
            pl.when(level == top)(chain)
        pl.when(level >= step)(functools.partial(attend, step))

    for j in (3, 1, 2, 0):
        for h in range(heads):
            total = jnp.sum(sum_buf[j * heads + h], axis=1, keepdims=True)
            o_buf[j, :, h * HEAD_DIM : (h + 1) * HEAD_DIM] = (
                acc_buf[j * heads + h] / total
            ).astype(BF16)
        if j > 0:
            o_copy(j, place).start()
    attn_ref[:, lanes(place * query_sets, query_sets)] = o_buf[0]

    for c in range(CHAIN):
        for j in range(1, GROUP):
            prefix_copy(c, j, peer_place[j]).wait_recv()
    square_own[...] = jnp.zeros(square_own.shape, F32)

    def gate_block(index, carry):
        columns = lanes(index * BLOCK, BLOCK)
        carried = jnp.dot(read_ref[...], start[:, columns], preferred_element_type=F32)
        gate = gate_ref[:, columns].astype(F32)
        mixed = part[:, columns] + expand_heads(jnp.exp(cum_ref[index])) * carried
        gated = mixed * (gate / (1.0 + jnp.exp(-gate)))
        part[:, columns] = gated
        square = gated * gated
        total = square_own[...]
        for k in range(BLOCK // 128):
            total = total + square[:, k * 128 : (k + 1) * 128]
        square_own[...] = total
        return carry

    lax.fori_loop(0, blocks, gate_block, 0)
    square_copy().start()
    square_copy().wait_recv()
    squares = jnp.sum(square_own[...] + square_other[...], axis=1, keepdims=True)
    row_scale = lax.rsqrt(squares / (SSM_HEADS * HEAD_P) + 1e-05)

    def norm_block(index, carry):
        columns = lanes(index * BLOCK, BLOCK)
        ssm_ref[:, columns] = (part[:, columns] * row_scale * gain_ref[:, columns]).astype(BF16)
        return carry

    lax.fori_loop(0, blocks, norm_block, 0)

    square_copy().wait_send()
    for j in range(1, GROUP):
        o_copy(j, peer_place[j]).wait_recv()
        o_copy(j, place).wait_send()
        q_copy(j).wait_send()
        for copy in kv_copies(j) + state_copies(j):
            copy.wait_send()
        for c in range(CHAIN):
            prefix_copy(c, j, place).wait_send()
    for step in range(groups - 1):

        @pl.when((level >= step) & (level < top))
        def _():
            for j in range(GROUP):
                up_copy(step, j).wait_send()

    @pl.when(level < top)
    def _():
        for c in range(CHAIN):
            chain_copy(c).wait_send()


def grouped_body(
    groups,
    ssm_input,
    gate_input,
    write_proj,
    read_proj,
    log_decay,
    skip_gain,
    norm_gain,
    query_rows,
    key_rows,
    value_rows,
):
    rows, width = ssm_input.shape
    steps = width // BLOCK
    quarter = width // GROUP
    causal = (jnp.arange(rows)[:, None] >= jnp.arange(rows)[None, :]).astype(F32)
    cum = jnp.dot(causal, log_decay, precision=lax.Precision.HIGHEST)
    cum_blocks = jnp.transpose(cum.reshape(rows, steps, WIDE), (1, 0, 2))
    cum_t = cum.T.reshape(steps, WIDE, rows)
    query_sets = query_rows.shape[1] // GROUP
    pairs = 2 * key_rows.shape[1] // GROUP
    heads = query_sets // HEAD_DIM
    piece = quarter // CHAIN
    vmem = pl.BlockSpec(memory_space=pltpu.VMEM)
    hbm = pl.BlockSpec(memory_space=pl.ANY)
    dma = pltpu.SemaphoreType.DMA
    others = GROUP - 1
    return pl.pallas_call(
        functools.partial(grouped_kernel, groups),
        in_specs=[hbm] * 11,
        out_specs=[vmem] * 2,
        out_shape=[
            jax.ShapeDtypeStruct((rows, width), BF16),
            jax.ShapeDtypeStruct(query_rows.shape, BF16),
        ],
        scratch_shapes=[
            pltpu.VMEM((rows, width), BF16),
            pltpu.VMEM((rows, width), BF16),
            pltpu.VMEM((rows, STATE), BF16),
            pltpu.VMEM((rows, STATE), BF16),
            pltpu.VMEM((steps, rows, WIDE), F32),
            pltpu.VMEM((steps, WIDE, rows), F32),
            pltpu.VMEM((1, width), F32),
            pltpu.VMEM((1, width), F32),
            pltpu.VMEM((groups, GROUP, rows, pairs), BF16),
            pltpu.VMEM((GROUP, rows, query_sets), BF16),
            pltpu.VMEM((GROUP, rows, query_sets), BF16),
            pltpu.VMEM((GROUP, STATE, quarter), BF16),
            pltpu.VMEM((GROUP, STATE, quarter), BF16),
            pltpu.VMEM((GROUP, 8, 128), F32),
            pltpu.VMEM((GROUP, 8, 128), F32),
            pltpu.VMEM((CHAIN, STATE, piece), BF16),
            pltpu.VMEM((CHAIN, STATE, piece), BF16),
            pltpu.VMEM((GROUP, CHAIN, STATE, piece), BF16),
            pltpu.VMEM((STATE, width), BF16),
            pltpu.VMEM((rows, width), F32),
            pltpu.VMEM((GROUP * heads, rows, HEAD_DIM), F32),
            pltpu.VMEM((GROUP * heads, rows, HEAD_DIM), F32),
            pltpu.VMEM((GROUP * heads, rows, HEAD_DIM), F32),
            pltpu.VMEM((rows, 128), F32),
            pltpu.VMEM((rows, 128), F32),
            dma((11,)),
            dma((2, others)),
            dma((2, others)),
            dma((others,)),
            dma((others,)),
            dma((others,)),
            dma((others,)),
            dma((others,)),
            dma((others,)),
            dma((groups - 1, GROUP)),
            dma((groups - 1, GROUP)),
            dma((CHAIN,)),
            dma((CHAIN,)),
            dma((CHAIN, others)),
            dma((CHAIN, others)),
            dma((others,)),
            dma((others,)),
            dma((1,)),
            dma((1,)),
        ],
        compiler_params=pltpu.CompilerParams(
            collective_id=0, has_side_effects=True, vmem_limit_bytes=50 * 2**20
        ),
        cost_estimate=pl.CostEstimate(
            flops=6 * 10**9, bytes_accessed=10 * 2**20, transcendentals=12 * 10**6
        ),
        name="hybrid_layers",
    )(
        ssm_input,
        gate_input,
        write_proj,
        read_proj,
        cum_blocks,
        cum_t,
        jnp.repeat(skip_gain, HEAD_P)[None],
        norm_gain[None],
        query_rows,
        key_rows,
        value_rows,
    )


def solution(mesh):
    in_specs = (
        P("ctx", "heads"),
        P("ctx", "heads"),
        P("ctx", None),
        P("ctx", None),
        P("ctx", "heads"),
        P("heads"),
        P("heads"),
        P("ctx", "heads"),
        P("ctx", "heads"),
        P("ctx", "heads"),
    )
    out_specs = (P("ctx", "heads"), P("ctx", "heads"))
    ctx, heads = mesh.shape["ctx"], mesh.shape["heads"]
    grouped = ctx % GROUP == 0 and ctx > GROUP and KV_HEADS // heads == GROUP and heads == 2
    chosen = functools.partial(grouped_body, ctx // GROUP) if grouped else body
    return jax.shard_map(chosen, mesh=mesh, in_specs=in_specs, out_specs=out_specs, check_vma=False)
```

```python
import functools
import math

import jax
import jax.numpy as jnp
from jax import lax
from jax.experimental import pallas as pl
from jax.experimental.pallas import tpu as pltpu
from jax.sharding import PartitionSpec as P

SSM_HEADS = 128
HEAD_P = 64
STATE = 128
QUERY_HEADS = 32
KV_HEADS = 8
HEAD_DIM = 128
SPAN = 64


def carried_in(part, axis, combine, identity):
    place = lax.axis_index(axis)
    gathered = jax.tree.map(lambda a: lax.all_gather(a, axis), part)
    state = jax.tree.map(lambda a, e: jnp.zeros_like(a) + jnp.asarray(e, a.dtype), part, identity)

    def one(step, state):
        return combine(
            state, jax.tree.map(lambda a: lax.dynamic_index_in_dim(a, step, 0, False), gathered)
        )

    return lax.fori_loop(0, place, one, state)


def chain_combine(earlier, later):
    return (earlier[0] * later[0], later[0][:, None, None] * earlier[1] + later[1])


def local_mixer(ssm_input, gate_input, write_proj, read_proj, log_decay, skip_gain, norm_gain):
    row_count, width_local = ssm_input.shape
    head_local = log_decay.shape[1]
    block_count = row_count // SPAN
    inputs_blk = ssm_input.reshape(block_count, SPAN, head_local, HEAD_P)
    inputs_float = inputs_blk.astype(jnp.float32)
    write_blk = write_proj.reshape(block_count, SPAN, STATE)
    read_blk = read_proj.reshape(block_count, SPAN, STATE)
    cum_decay = jnp.cumsum(log_decay.reshape(block_count, SPAN, head_local), axis=1)
    cum_heads = jnp.transpose(cum_decay, (0, 2, 1))
    causal = jnp.arange(SPAN)[:, None] >= jnp.arange(SPAN)[None, :]
    decay_gap = cum_heads[:, :, :, None] - cum_heads[:, :, None, :]
    decay_mask = jnp.where(causal, jnp.exp(jnp.where(causal, decay_gap, 0.0)), 0.0)
    intersection = jnp.einsum(
        "ctn,csn->cts", read_blk, write_blk, preferred_element_type=jnp.float32
    )
    mix_weights = intersection[:, None] * decay_mask
    y_local = jnp.einsum(
        "chts,cshp->cthp", mix_weights, inputs_float, precision=lax.Precision.HIGHEST
    )
    tail_decay = jnp.exp(cum_heads[:, :, -1:] - cum_heads)
    weighted_write = tail_decay[:, :, :, None] * write_blk[:, None].astype(jnp.float32)
    block_state = jnp.einsum(
        "cshp,chsn->chpn", inputs_float, weighted_write, precision=lax.Precision.HIGHEST
    )
    block_decay = jnp.exp(cum_heads[:, :, -1])

    def prefix_step(carry_in, block_item):
        return (chain_combine(carry_in, block_item), carry_in)

    start_pair = (
        jnp.ones((head_local,), jnp.float32),
        jnp.zeros((head_local, HEAD_P, STATE), jnp.float32),
    )
    device_pair, prefix_pair = lax.scan(prefix_step, start_pair, (block_decay, block_state))
    incoming = carried_in(device_pair, "ctx", chain_combine, start_pair)
    start_state = prefix_pair[0][:, :, None, None] * incoming[1][None] + prefix_pair[1]
    y_carry = (
        jnp.einsum(
            "ctn,chpn->cthp",
            read_blk.astype(jnp.float32),
            start_state,
            precision=lax.Precision.HIGHEST,
        )
        * jnp.exp(cum_decay)[:, :, :, None]
    )
    mixed_out = y_local + y_carry + skip_gain[None, None, :, None] * inputs_float
    gated = mixed_out.reshape(row_count, width_local) * jax.nn.silu(gate_input.astype(jnp.float32))
    square_total = lax.psum(jnp.sum(gated * gated, axis=1), "heads")
    row_scale = lax.rsqrt(square_total / (SSM_HEADS * HEAD_P) + 1e-05)
    return (gated * row_scale[:, None] * norm_gain[None, :]).astype(jnp.bfloat16)


def attend_block(
    state, query_block, query_positions, top_position, key_block, value_block, first_key
):
    scale_factor = 1.0 / HEAD_DIM**0.5
    key_count = key_block.shape[0]

    def compute(state_in):
        running_max, running_sum, running_acc = state_in
        scores = (
            jnp.einsum("gqd,ngd->gqn", query_block, key_block, preferred_element_type=jnp.float32)
            * scale_factor
        )
        key_positions = first_key + jnp.arange(key_count, dtype=jnp.int32)
        visible = key_positions[None, None, :] <= query_positions[None, :, None]
        block_max = jnp.max(jnp.where(visible, scores, -1e30), axis=2)
        new_max = jnp.maximum(running_max, block_max)
        weights = jnp.where(
            visible, jnp.exp(jnp.where(visible, scores - new_max[:, :, None], 0.0)), 0.0
        )
        rescale = jnp.exp(running_max - new_max)
        new_sum = rescale * running_sum + jnp.sum(weights, axis=2)
        new_acc = rescale[:, :, None] * running_acc + jnp.einsum(
            "gqn,ngd->gqd",
            weights.astype(jnp.bfloat16),
            value_block,
            preferred_element_type=jnp.float32,
        )
        return (new_max, new_sum, new_acc)

    return lax.cond(first_key > top_position, lambda state_in: state_in, compute, state)


def attention_local(query_rows, key_rows, value_rows):
    row_count = query_rows.shape[0]
    head_sets = key_rows.shape[1] // HEAD_DIM
    group_size = QUERY_HEADS // KV_HEADS
    own_index = lax.axis_index("ctx")
    query_stack = query_rows.reshape(row_count, head_sets, group_size, HEAD_DIM)
    query_stack = jnp.transpose(query_stack, (1, 0, 2, 3)).reshape(
        head_sets, row_count * group_size, HEAD_DIM
    )
    stacked_rows = jnp.arange(row_count * group_size, dtype=jnp.int32) // group_size
    own_positions = own_index * row_count + stacked_rows
    query_sets = [(query_stack, own_positions)]
    tops = [jnp.max(positions) for _, positions in query_sets]
    carries = tuple(
        (
            (
                jnp.full((head_sets, block.shape[1]), -1e30, jnp.float32),
                jnp.zeros((head_sets, block.shape[1]), jnp.float32),
                jnp.zeros((head_sets, block.shape[1], HEAD_DIM), jnp.float32),
            )
            for block, _ in query_sets
        )
    )
    key_piece = lax.all_gather(key_rows, "ctx", axis=0, tiled=True)
    value_piece = lax.all_gather(value_rows, "ctx", axis=0, tiled=True)
    piece_rows = key_piece.shape[0]
    key_blocks = key_piece.reshape(piece_rows // row_count, row_count, head_sets, HEAD_DIM)
    value_blocks = value_piece.reshape(piece_rows // row_count, row_count, head_sets, HEAD_DIM)
    offsets = row_count * jnp.arange(piece_rows // row_count, dtype=jnp.int32)

    def inner_step(states, block_item):
        key_block, value_block, first_key = block_item
        updated = tuple(
            (
                attend_block(
                    states[number],
                    query_sets[number][0],
                    query_sets[number][1],
                    tops[number],
                    key_block,
                    value_block,
                    first_key,
                )
                for number in range(len(query_sets))
            )
        )
        return (updated, None)

    result, _ = lax.scan(inner_step, carries, (key_blocks, value_blocks, offsets))
    finished = [(state[2] / state[1][:, :, None]).astype(jnp.bfloat16) for state in result]
    combined = finished[0]
    combined = combined.reshape(head_sets, row_count, group_size, HEAD_DIM)
    return jnp.transpose(combined, (1, 0, 2, 3)).reshape(
        row_count, head_sets * group_size * HEAD_DIM
    )


def body(
    ssm_input,
    gate_input,
    write_proj,
    read_proj,
    log_decay,
    skip_gain,
    norm_gain,
    query_rows,
    key_rows,
    value_rows,
):
    ssm_out = local_mixer(
        ssm_input, gate_input, write_proj, read_proj, log_decay, skip_gain, norm_gain
    )
    attn_out = attention_local(query_rows, key_rows, value_rows)
    return (ssm_out, attn_out)


GROUP = 4
WIDE = 8
BLOCK = WIDE * HEAD_P
CHAIN = 4
F32 = jnp.float32
BF16 = jnp.bfloat16
LOG2E = math.log2(math.e)
MESH = pl.DeviceIdType.MESH


def xor_place(a, b):
    a1, a0, b1, b0 = a // 2, a % 2, b // 2, b % 2
    return 2 * (a1 + b1 - 2 * a1 * b1) + (a0 + b0 - 2 * a0 * b0)


def lanes(start, size):
    return pl.ds(pl.multiple_of(start, 128), size)


def spread_heads(per_head):
    first = lax.broadcasted_iota(jnp.int32, (WIDE, BLOCK), 0) * HEAD_P
    column = lax.broadcasted_iota(jnp.int32, (WIDE, BLOCK), 1)
    spread = jnp.where((column >= first) & (column < first + HEAD_P), 1.0, 0.0).astype(BF16)
    return jnp.dot(per_head.astype(BF16), spread, preferred_element_type=F32)


def expand_heads(per_head):
    high = per_head.astype(BF16)
    return spread_heads(high) + spread_heads(per_head - high.astype(F32))


def grouped_kernel(
    groups,
    x_hbm,
    gate_hbm,
    write_hbm,
    read_hbm,
    cum_hbm,
    cum_t_hbm,
    skip_hbm,
    gain_hbm,
    query_ref,
    key_ref,
    value_ref,
    ssm_ref,
    attn_ref,
    x_ref,
    gate_ref,
    write_ref,
    read_ref,
    cum_ref,
    cum_t_ref,
    skip_ref,
    gain_ref,
    kv_buf,
    q_buf,
    o_buf,
    own_states,
    states,
    own_decays,
    decays,
    carry_in,
    carry_out,
    prefix,
    start,
    part,
    top_buf,
    sum_buf,
    acc_buf,
    square_own,
    square_other,
    load_sem,
    kv_send,
    kv_recv,
    q_send,
    q_recv,
    state_send,
    state_recv,
    decay_send,
    decay_recv,
    up_send,
    up_recv,
    chain_send,
    chain_recv,
    prefix_send,
    prefix_recv,
    o_send,
    o_recv,
    square_send,
    square_recv,
):
    rows, width = x_ref.shape
    quarter = width // GROUP
    blocks = width // BLOCK
    own = lax.axis_index("ctx")
    place, level = own % GROUP, own // GROUP
    top = groups - 1
    base = level * GROUP
    peer_place = [xor_place(place, j) for j in range(GROUP)]
    other = 1 - lax.axis_index("heads")

    def remote(src, dst, send, recv, **device):
        return pltpu.make_async_remote_copy(
            src_ref=src,
            dst_ref=dst,
            send_sem=send,
            recv_sem=recv,
            device_id=device,
            device_id_type=MESH,
        )

    def to_peer(j, src, dst, send, recv):
        return remote(src, dst, send, recv, ctx=base + peer_place[j])

    key_sets = key_ref.shape[1] // GROUP
    query_sets = query_ref.shape[1] // GROUP

    def kv_copies(j):
        columns = lanes(peer_place[j] * key_sets, key_sets)
        return [
            to_peer(
                j,
                ref.at[:, columns],
                kv_buf.at[0, j, :, pl.ds(k * key_sets, key_sets)],
                kv_send.at[k, j - 1],
                kv_recv.at[k, j - 1],
            )
            for k, ref in enumerate((key_ref, value_ref))
        ]

    def q_copy(j):
        columns = lanes(peer_place[j] * query_sets, query_sets)
        return to_peer(
            j, query_ref.at[:, columns], q_buf.at[j], q_send.at[j - 1], q_recv.at[j - 1]
        )

    def state_copies(j):
        return [
            to_peer(
                j, own_states.at[j], states.at[j], state_send.at[j - 1], state_recv.at[j - 1]
            ),
            to_peer(
                j, own_decays.at[j], decays.at[j], decay_send.at[j - 1], decay_recv.at[j - 1]
            ),
        ]

    def up_copy(step, j):
        return remote(
            kv_buf.at[step, j],
            kv_buf.at[step + 1, j],
            up_send.at[step, j],
            up_recv.at[step, j],
            ctx=lax.rem(own + GROUP, groups * GROUP),
        )

    piece = quarter // CHAIN

    def chain_copy(c):
        return remote(
            carry_out.at[c],
            carry_in.at[c],
            chain_send.at[c],
            chain_recv.at[c],
            ctx=lax.rem(own + GROUP, groups * GROUP),
        )

    def prefix_copy(c, j, landing):
        return to_peer(
            j,
            prefix.at[peer_place[j], c],
            start.at[:, lanes(landing * quarter + c * piece, piece)],
            prefix_send.at[c, j - 1],
            prefix_recv.at[c, j - 1],
        )

    def o_copy(j, landing):
        return to_peer(
            j,
            o_buf.at[j],
            attn_ref.at[:, lanes(landing * query_sets, query_sets)],
            o_send.at[j - 1],
            o_recv.at[j - 1],
        )

    def square_copy():
        return remote(square_own, square_other, square_send.at[0], square_recv.at[0], heads=other)

    def loads():
        own_keys = lanes(place * key_sets, key_sets)
        pairs = [
            (x_hbm, x_ref),
            (cum_hbm, cum_ref),
            (write_hbm, write_ref),
            (read_hbm, read_ref),
            (cum_t_hbm, cum_t_ref),
            (skip_hbm, skip_ref),
            (gain_hbm, gain_ref),
            (key_ref.at[:, own_keys], kv_buf.at[0, 0, :, pl.ds(0, key_sets)]),
            (value_ref.at[:, own_keys], kv_buf.at[0, 0, :, pl.ds(key_sets, key_sets)]),
            (query_ref.at[:, lanes(place * query_sets, query_sets)], q_buf.at[0]),
            (gate_hbm, gate_ref),
        ]
        return [
            pltpu.make_async_copy(src, dst, load_sem.at[n]) for n, (src, dst) in enumerate(pairs)
        ]

    for copy in loads():
        copy.start()

    barrier = pltpu.get_barrier_semaphore()
    for j in range(1, GROUP):
        pl.semaphore_signal(
            barrier, inc=1, device_id={"ctx": base + peer_place[j]}, device_id_type=MESH
        )
    pl.semaphore_signal(barrier, inc=1, device_id={"heads": other}, device_id_type=MESH)

    for step in (GROUP, (groups - 1) * GROUP):
        neighbour = lax.rem(own + step, groups * GROUP)
        pl.semaphore_signal(barrier, inc=1, device_id={"ctx": neighbour}, device_id_type=MESH)
    pl.semaphore_wait(barrier, GROUP + 2)

    for j in range(1, GROUP):
        for copy in kv_copies(j):
            copy.start()
    for j in range(1, GROUP):
        q_copy(j).start()
    for copy in loads()[:3]:
        copy.wait()

    def state_block(j, b):
        index = peer_place[j] * (quarter // BLOCK) + b
        cum = cum_ref[index]
        last = cum[rows - 1 :, :]
        weight = spread_heads(jnp.exp(last - cum)).astype(BF16)
        scaled = x_ref[:, lanes(index * BLOCK, BLOCK)] * weight
        state = lax.dot_general(
            write_ref[...], scaled, (((0,), (0,)), ((), ())), preferred_element_type=F32
        )
        columns = slice(b * BLOCK, (b + 1) * BLOCK)
        if j == 0:
            states[0, :, columns] = state.astype(BF16)
            decays[0, b : b + 1, 0:WIDE] = last
        else:
            own_states[j, :, columns] = state.astype(BF16)
            own_decays[j, b : b + 1, 0:WIDE] = last

    own_decays[...] = jnp.zeros(own_decays.shape, F32)
    for j in (3, 1, 2, 0):
        for b in range(quarter // BLOCK):
            state_block(j, b)
        if j > 0:
            for copy in state_copies(j):
                copy.start()

    def forward(step):
        if step < groups - 1:

            @pl.when((level >= step) & (level < top))
            def _():
                for j in range(GROUP):
                    if step > 0:
                        up_copy(step - 1, j).wait_recv()
                    up_copy(step, j).start()

        if step > 0:

            @pl.when((level >= step) & (level == top))
            def _():
                for j in range(GROUP):
                    up_copy(step - 1, j).wait_recv()

    for copy in loads()[3:]:
        copy.wait()

    inner = lax.dot_general(
        read_ref[...], write_ref[...], (((1,), (1,)), ((), ())), preferred_element_type=F32
    )
    later = lax.broadcasted_iota(jnp.int32, (rows, rows), 0)
    earlier = lax.broadcasted_iota(jnp.int32, (rows, rows), 1)
    inner = jnp.where(earlier <= later, inner, 0.0)
    left = lax.broadcasted_iota(jnp.int32, (rows, 2 * HEAD_P), 1) < HEAD_P

    def local_block(index, carry):
        cum = cum_ref[index]
        cum_t = cum_t_ref[index]
        for pair in range(WIDE // 2):
            columns = lanes(index * BLOCK + pair * 2 * HEAD_P, 2 * HEAD_P)
            x_pair = x_ref[:, columns]
            halves = []
            for h in (2 * pair, 2 * pair + 1):
                gap = cum[:, h : h + 1] - cum_t[h : h + 1, :]
                mix = (jnp.exp(jnp.minimum(gap, 0.0)) * inner).astype(BF16)
                halves.append(jnp.dot(mix, x_pair, preferred_element_type=F32))
            mixed = jnp.where(left, halves[0], halves[1])
            part[:, columns] = mixed + skip_ref[:, columns] * x_pair.astype(F32)
        return carry

    lax.fori_loop(0, blocks // 2, local_block, 0)
    for j in range(1, GROUP):
        for copy in kv_copies(j):
            copy.wait_recv()
    forward(0)
    lax.fori_loop(blocks // 2, blocks, local_block, 0)

    def chain():
        for j in range(1, GROUP):
            for copy in state_copies(j):
                copy.wait_recv()
        passed = [
            [
                expand_heads(
                    jnp.exp(
                        jnp.broadcast_to(
                            decays[xor_place(place, k), b : b + 1, 0:WIDE], (8, WIDE)
                        )
                    )
                )[0:1, :]
                for b in range(quarter // BLOCK)
            ]
            for k in range(GROUP)
        ]
        for c in range(CHAIN):
            columns = slice(c * piece, (c + 1) * piece)

            @pl.when(level > 0)
            def _():
                chain_copy(c).wait_recv()

            @pl.when(level == 0)
            def _():
                carry_in[c] = jnp.zeros(carry_in.shape[1:], BF16)

            state = carry_in[c].astype(F32)
            for k in range(GROUP):
                prefix[k, c] = state.astype(BF16)
                j = xor_place(place, k)
                at = c * piece % BLOCK
                decay = passed[k][c * piece // BLOCK][:, at : at + piece]
                state = decay * state + states[j, :, columns].astype(F32)
            carry_out[c] = state.astype(BF16)

            @pl.when(level < top)
            def _():
                chain_copy(c).start()

            for j in range(1, GROUP):
                prefix_copy(c, j, place).start()
            start[:, lanes(place * quarter + c * piece, piece)] = prefix[place, c]

    factor = LOG2E / math.sqrt(HEAD_DIM)
    heads = query_sets // HEAD_DIM
    key_count = GROUP * rows

    def own_blocks(count):
        keys_values = [kv_buf[0, xor_place(place, k)] for k in range(count)]
        return jnp.concatenate(keys_values) if count > 1 else keys_values[0]

    def attend_own():
        row = lax.broadcasted_iota(jnp.int32, (rows, 1), 0)
        for block in range(GROUP):
            entry = xor_place(place, block)
            keys_values = own_blocks(block + 1)
            keys, values = keys_values[:, :HEAD_DIM], keys_values[:, HEAD_DIM:]
            key_total = (block + 1) * rows
            visible = (
                lax.broadcasted_iota(jnp.int32, (rows, key_total), 1) <= row + block * rows
            )
            for h in range(heads):
                query = q_buf[entry, :, h * HEAD_DIM : (h + 1) * HEAD_DIM]
                scores = lax.dot_general(
                    query, keys, (((1,), (1,)), ((), ())), preferred_element_type=F32
                )
                scores = jnp.where(visible, scores, -1e30)
                new_max = jnp.max(scores, axis=1, keepdims=True)
                weights = jnp.exp2((scores - new_max) * factor)
                total = jnp.sum(weights, axis=1, keepdims=True)
                lane = lax.broadcasted_iota(jnp.int32, (rows, HEAD_DIM), 1)
                at = entry * heads + h
                top_buf[at] = jnp.broadcast_to(new_max, (rows, HEAD_DIM))
                sum_buf[at] = jnp.where(lane == 0, total, 0.0)
                acc_buf[at] = jnp.dot(weights.astype(BF16), values, preferred_element_type=F32)

    def attend(step):
        keys = kv_buf[step, :, :, 0:HEAD_DIM].reshape(key_count, HEAD_DIM)
        values = kv_buf[step, :, :, HEAD_DIM:].reshape(key_count, HEAD_DIM)

        def one(block, carry):
            query = jnp.concatenate(
                [q_buf[block, :, h * HEAD_DIM : (h + 1) * HEAD_DIM] for h in range(heads)]
            )
            at = pl.ds(block * heads, heads)
            stacked = (heads * rows, HEAD_DIM)
            old_max = top_buf[at].reshape(stacked)
            scores = lax.dot_general(
                query, keys, (((1,), (1,)), ((), ())), preferred_element_type=F32
            )
            new_max = jnp.maximum(jnp.max(scores, axis=1, keepdims=True), old_max[:, :1])
            weights = jnp.exp2((scores - new_max) * factor)
            new_sum = weights[:, :HEAD_DIM]
            for k in range(1, key_count // HEAD_DIM):
                new_sum = new_sum + weights[:, k * HEAD_DIM : (k + 1) * HEAD_DIM]
            new_acc = jnp.dot(weights.astype(BF16), values, preferred_element_type=F32)
            rescale = jnp.exp2((old_max - new_max) * factor)
            new_sum = new_sum + rescale * sum_buf[at].reshape(stacked)
            new_acc = new_acc + rescale * acc_buf[at].reshape(stacked)
            shape = (heads, rows, HEAD_DIM)
            top_buf[at] = jnp.broadcast_to(new_max, stacked).reshape(shape)
            sum_buf[at] = new_sum.reshape(shape)
            acc_buf[at] = new_acc.reshape(shape)
            return carry

        lax.fori_loop(0, GROUP, one, 0)

    for j in range(1, GROUP):
        q_copy(j).wait_recv()
    attend_own()
    pl.when(level == 0)(chain)
    for step in range(1, groups):
        forward(step)
        if step < groups - 1:
            pl.when(level == step)(chain)
        else:
            pl.when(level == top)(chain)
        pl.when(level >= step)(functools.partial(attend, step))

    for j in (3, 1, 2, 0):
        for h in range(heads):
            total = jnp.sum(sum_buf[j * heads + h], axis=1, keepdims=True)
            o_buf[j, :, h * HEAD_DIM : (h + 1) * HEAD_DIM] = (
                acc_buf[j * heads + h] / total
            ).astype(BF16)
        if j > 0:
            o_copy(j, place).start()
    attn_ref[:, lanes(place * query_sets, query_sets)] = o_buf[0]

    square_own[...] = jnp.zeros(square_own.shape, F32)

    def gate_block(index, carry):
        columns = lanes(index * BLOCK, BLOCK)
        carried = jnp.dot(read_ref[...], start[:, columns], preferred_element_type=F32)
        gate = gate_ref[:, columns].astype(F32)
        mixed = part[:, columns] + expand_heads(jnp.exp(cum_ref[index])) * carried
        gated = mixed * (gate / (1.0 + jnp.exp(-gate)))
        part[:, columns] = gated
        square = gated * gated
        total = square_own[...]
        for k in range(BLOCK // 128):
            total = total + square[:, k * 128 : (k + 1) * 128]
        square_own[...] = total
        return carry

    for j in range(GROUP):
        if j > 0:
            for c in range(CHAIN):
                prefix_copy(c, j, peer_place[j]).wait_recv()
        first = peer_place[j] * (quarter // BLOCK)
        for b in range(quarter // BLOCK):
            gate_block(first + b, 0)
    square_copy().start()
    square_copy().wait_recv()
    squares = jnp.sum(square_own[...] + square_other[...], axis=1, keepdims=True)
    row_scale = lax.rsqrt(squares / (SSM_HEADS * HEAD_P) + 1e-05)

    def norm_block(index, carry):
        columns = lanes(index * BLOCK, BLOCK)
        ssm_ref[:, columns] = (part[:, columns] * row_scale * gain_ref[:, columns]).astype(BF16)
        return carry

    lax.fori_loop(0, blocks, norm_block, 0)

    square_copy().wait_send()
    for j in range(1, GROUP):
        o_copy(j, peer_place[j]).wait_recv()
        o_copy(j, place).wait_send()
        q_copy(j).wait_send()
        for copy in kv_copies(j) + state_copies(j):
            copy.wait_send()
        for c in range(CHAIN):
            prefix_copy(c, j, place).wait_send()
    for step in range(groups - 1):

        @pl.when((level >= step) & (level < top))
        def _():
            for j in range(GROUP):
                up_copy(step, j).wait_send()

    @pl.when(level < top)
    def _():
        for c in range(CHAIN):
            chain_copy(c).wait_send()


def grouped_body(
    groups,
    ssm_input,
    gate_input,
    write_proj,
    read_proj,
    log_decay,
    skip_gain,
    norm_gain,
    query_rows,
    key_rows,
    value_rows,
):
    rows, width = ssm_input.shape
    steps = width // BLOCK
    quarter = width // GROUP
    causal = (jnp.arange(rows)[:, None] >= jnp.arange(rows)[None, :]).astype(F32)
    cum = jnp.dot(causal, log_decay, precision=lax.Precision.HIGHEST)
    cum_blocks = jnp.transpose(cum.reshape(rows, steps, WIDE), (1, 0, 2))
    cum_t = cum.T.reshape(steps, WIDE, rows)
    query_sets = query_rows.shape[1] // GROUP
    pairs = 2 * key_rows.shape[1] // GROUP
    heads = query_sets // HEAD_DIM
    piece = quarter // CHAIN
    vmem = pl.BlockSpec(memory_space=pltpu.VMEM)
    hbm = pl.BlockSpec(memory_space=pltpu.HBM)
    dma = pltpu.SemaphoreType.DMA
    others = GROUP - 1
    return pl.pallas_call(
        functools.partial(grouped_kernel, groups),
        in_specs=[hbm] * 11,
        out_specs=[vmem] * 2,
        out_shape=[
            jax.ShapeDtypeStruct((rows, width), BF16),
            jax.ShapeDtypeStruct(query_rows.shape, BF16),
        ],
        scratch_shapes=[
            pltpu.VMEM((rows, width), BF16),
            pltpu.VMEM((rows, width), BF16),
            pltpu.VMEM((rows, STATE), BF16),
            pltpu.VMEM((rows, STATE), BF16),
            pltpu.VMEM((steps, rows, WIDE), F32),
            pltpu.VMEM((steps, WIDE, rows), F32),
            pltpu.VMEM((1, width), F32),
            pltpu.VMEM((1, width), F32),
            pltpu.VMEM((groups, GROUP, rows, pairs), BF16),
            pltpu.VMEM((GROUP, rows, query_sets), BF16),
            pltpu.VMEM((GROUP, rows, query_sets), BF16),
            pltpu.VMEM((GROUP, STATE, quarter), BF16),
            pltpu.VMEM((GROUP, STATE, quarter), BF16),
            pltpu.VMEM((GROUP, 8, 128), F32),
            pltpu.VMEM((GROUP, 8, 128), F32),
            pltpu.VMEM((CHAIN, STATE, piece), BF16),
            pltpu.VMEM((CHAIN, STATE, piece), BF16),
            pltpu.VMEM((GROUP, CHAIN, STATE, piece), BF16),
            pltpu.VMEM((STATE, width), BF16),
            pltpu.VMEM((rows, width), F32),
            pltpu.VMEM((GROUP * heads, rows, HEAD_DIM), F32),
            pltpu.VMEM((GROUP * heads, rows, HEAD_DIM), F32),
            pltpu.VMEM((GROUP * heads, rows, HEAD_DIM), F32),
            pltpu.VMEM((rows, 128), F32),
            pltpu.VMEM((rows, 128), F32),
            dma((11,)),
            dma((2, others)),
            dma((2, others)),
            dma((others,)),
            dma((others,)),
            dma((others,)),
            dma((others,)),
            dma((others,)),
            dma((others,)),
            dma((groups - 1, GROUP)),
            dma((groups - 1, GROUP)),
            dma((CHAIN,)),
            dma((CHAIN,)),
            dma((CHAIN, others)),
            dma((CHAIN, others)),
            dma((others,)),
            dma((others,)),
            dma((1,)),
            dma((1,)),
        ],
        compiler_params=pltpu.CompilerParams(
            collective_id=0, has_side_effects=True, vmem_limit_bytes=50 * 2**20
        ),
        cost_estimate=pl.CostEstimate(
            flops=6 * 10**9, bytes_accessed=10 * 2**20, transcendentals=12 * 10**6
        ),
        name="hybrid_layers",
    )(
        ssm_input,
        gate_input,
        write_proj,
        read_proj,
        cum_blocks,
        cum_t,
        jnp.repeat(skip_gain, HEAD_P)[None],
        norm_gain[None],
        query_rows,
        key_rows,
        value_rows,
    )


def solution(mesh):
    in_specs = (
        P("ctx", "heads"),
        P("ctx", "heads"),
        P("ctx", None),
        P("ctx", None),
        P("ctx", "heads"),
        P("heads"),
        P("heads"),
        P("ctx", "heads"),
        P("ctx", "heads"),
        P("ctx", "heads"),
    )
    out_specs = (P("ctx", "heads"), P("ctx", "heads"))
    ctx, heads = mesh.shape["ctx"], mesh.shape["heads"]
    grouped = ctx % GROUP == 0 and ctx > GROUP and KV_HEADS // heads == GROUP and heads == 2
    chosen = functools.partial(grouped_body, ctx // GROUP) if grouped else body
    return jax.shard_map(chosen, mesh=mesh, in_specs=in_specs, out_specs=out_specs, check_vma=False)
```
